256 devices in a mesh: frame: 32 (over x_hi, z, core), space: 8 (over y, x_lo).
Axes of the slice: x: 4 (x_hi: 2, x_lo: 2; x = x_hi * 2 + x_lo), y: 4, z: 8, core: 2. Of those that a mesh axis runs over, the one named last changes fastest.
Arguments:
- latents: float32 [64, 1024, 16], P('frame', 'space'), may hold values from -6 to 6
- fresh_noise: float32 [1, 1024, 16], P(None, 'space'), may hold values from -6 to 6
- levels: int32 [64], P('frame'), may hold values from 1 to 64, as said below
- timesteps: int32 [65], replicated, may hold values from 0 to 1000, as said below
- window_offsets: int32 [2], replicated, may hold values from 0 to 15
- time_proj: bfloat16 [256, 6912], replicated, may hold values from -0.1875 to 0.1875
- embed_in: bfloat16 [16, 1152], replicated, may hold values from -1.5 to 1.5
- spatial_proj: bfloat16 [1152, 3456], P('frame'), may hold values from -0.1875 to 0.1875
- spatial_out: bfloat16 [1152, 1152], P('frame'), may hold values from -0.1875 to 0.1875
- temporal_proj: bfloat16 [1152, 3456], P('frame'), may hold values from -0.1875 to 0.1875
- temporal_out: bfloat16 [1152, 1152], P('frame'), may hold values from -0.1875 to 0.1875
- embed_out: bfloat16 [1152, 16], replicated, may hold values from -0.1875 to 0.1875
Outputs:
- queue: float32 [64, 1024, 16], P('frame', 'space')
- velocity: float32 [2, 64, 1024, 16], P(None, 'frame', 'space')
The draws below stay inside these ranges and needn't reach their ends.
Inputs may be any that keep to these rules, and one draw needn't show every extreme that they name: `levels`: non-decreasing along the queue; the first position has level 1 and the last level 64. `timesteps`: strictly increasing, the first entry 0 and the last 1000.
All inputs are finite; a program needn't handle non-finite values.
Results may differ from the reference program's by a relative error of at most 0.008.
Values may be sent and summed in bfloat16 or wider, within the bound.
A program may use at most 128 MiB of HBM per device.

```python
import math
import jax
import jax.numpy as jnp
from jax import lax

D = 1152
HEADS = 16
HEAD = 72
PATCH_IN = 16
FREQ = 256
WIN = 16
LEVELS = 64
STEPS = 2
FRAMES = 64
TOKF = 1024


def draw_levels(key, part):
    key = jax.random.fold_in(key, 11)
    raw = jax.random.randint(key, (FRAMES,), 1, LEVELS + 1)
    ordered = jnp.sort(raw)
    ordered = ordered.at[0].set(1).at[FRAMES - 1].set(LEVELS)
    return ordered.astype(jnp.int32)


def draw_timesteps(key, part):
    key = jax.random.fold_in(key, 23)
    rises = jax.random.randint(key, (LEVELS,), 8, 16)
    table = jnp.concatenate([jnp.zeros((1,), jnp.int32), jnp.cumsum(rises).astype(jnp.int32)])
    table = table.at[LEVELS].set(1000)
    return table.astype(jnp.int32)


def block_scale(rng, shape, cuts, low, largest):
    factor_of, own = 1.0, jax.random.fold_in(rng, 6)
    for position, parts in cuts:
        draws = jnp.exp(jax.random.uniform(jax.random.fold_in(own, position), (parts,), jnp.float32, low / len(cuts), largest / len(cuts)))
        factor_of = factor_of * jnp.repeat(draws, shape[position] // parts).reshape([-1 if axis == position else 1 for axis in range(len(shape))])
    return factor_of


def normal_values(key, shape, width, limit, cuts=(), kind=jnp.bfloat16):
    loudness = block_scale(key, shape, cuts, -0.22, 0.18) if cuts else 1.0
    values = jax.random.normal(key, shape, jnp.float32) * width * loudness
    return jnp.minimum(jnp.maximum(values, -limit), limit).astype(kind)


def setup_inputs(seed: int = 0) -> dict:
    key_of = jax.random.split(jax.random.key(seed), 13)
    latents = normal_values(key_of[0], (FRAMES, TOKF, PATCH_IN), 1.0, 6.0, ((0, 32), (1, 8)), jnp.float32)
    fresh_noise = normal_values(key_of[1], (STEPS - 1, TOKF, PATCH_IN), 1.0, 6.0, ((1, 8),), jnp.float32)
    levels = draw_levels(jax.random.fold_in(key_of[12], 71), 0)
    timesteps = draw_timesteps(jax.random.fold_in(key_of[12], 71), 0)
    window_offsets = jax.random.randint(key_of[4], (STEPS,), 0, WIN).astype(jnp.int32)
    time_proj = normal_values(key_of[5], (FREQ, 6 * D), (4 * FREQ) ** -0.5, 0.1875)
    embed_in = normal_values(key_of[6], (PATCH_IN, D), PATCH_IN ** -0.5, 1.5)
    spatial_proj = normal_values(key_of[7], (D, 3 * D), D ** -0.5, 0.1875, ((0, 32),))
    spatial_out = normal_values(key_of[8], (D, D), D ** -0.5, 0.1875, ((0, 32),))
    temporal_proj = normal_values(key_of[9], (D, 3 * D), D ** -0.5, 0.1875, ((0, 32),))
    temporal_out = normal_values(key_of[10], (D, D), D ** -0.5, 0.1875, ((0, 32),))
    embed_out = normal_values(key_of[11], (D, PATCH_IN), D ** -0.5, 0.1875)
    return {"latents": latents, "fresh_noise": fresh_noise, "levels": levels, "timesteps": timesteps, "window_offsets": window_offsets, "time_proj": time_proj, "embed_in": embed_in, "spatial_proj": spatial_proj, "spatial_out": spatial_out, "temporal_proj": temporal_proj, "temporal_out": temporal_out, "embed_out": embed_out}


epsilon = 1e-06

def layer_norm(values):
    center = values - lax.optimization_barrier(jnp.mean(values, -1, keepdims=True))
    spread = lax.optimization_barrier(jnp.mean(center * center, -1, keepdims=True))
    return center * lax.rsqrt(spread + epsilon)

def head_norm(values):
    return values * lax.rsqrt(lax.optimization_barrier(jnp.mean(values * values, -1, keepdims=True)) + epsilon)

def rounded_norm(values):
    return lax.optimization_barrier(head_norm(values).astype(jnp.bfloat16)).astype(jnp.float32)

def time_modulation(time_value, time_proj):
    half = time_proj.shape[0] // 2
    freqs = jnp.exp(-math.log(10000.0) * jnp.arange(half, dtype=jnp.float32) / half)
    angles = time_value[:, None] * freqs[None, :]
    features = jnp.concatenate([jnp.cos(angles), jnp.sin(angles)], -1).astype(jnp.bfloat16)
    return jnp.dot(features, time_proj, preferred_element_type=jnp.float32)

def softmax_rows(scores):
    raised = jnp.exp(scores)
    return (raised / lax.optimization_barrier(jnp.sum(raised, -1, keepdims=True))).astype(jnp.bfloat16)

def spatial_frame(triple):
    tokens = triple.shape[0]
    split = triple.reshape(tokens, 3, HEADS, HEAD).astype(jnp.float32)
    queries = rounded_norm(split[:, 0])
    keys = rounded_norm(split[:, 1])
    scores = jnp.einsum('qhd,khd->hqk', queries, keys) * HEAD ** (-0.5)
    weights = softmax_rows(scores).astype(jnp.float32)
    mixed = jnp.einsum('hqk,khd->qhd', weights, split[:, 2])
    return mixed.astype(jnp.bfloat16).reshape(tokens, HEADS * HEAD)

def temporal_attention(triple, offset):
    frames, tokens = (triple.shape[0], triple.shape[1])
    split = triple.reshape(frames, tokens, 3, HEADS, HEAD).astype(jnp.float32)
    queries = rounded_norm(split[:, :, 0])
    keys = rounded_norm(split[:, :, 1])
    window = (jnp.arange(frames, dtype=jnp.int32) + WIN - offset) // WIN
    same = window[:, None] == window[None, :]
    scores = jnp.einsum('fthd,gthd->thfg', queries, keys) * HEAD ** (-0.5)
    scores = jnp.where(same[None, None], scores, -1e+30)
    weights = softmax_rows(scores).astype(jnp.float32)
    mixed = jnp.einsum('thfg,gthd->fthd', weights, split[:, :, 2])
    return mixed.astype(jnp.bfloat16).reshape(frames, tokens, HEADS * HEAD)

def reference(latents, fresh_noise, levels, timesteps, window_offsets, time_proj, embed_in, spatial_proj, spatial_out, temporal_proj, temporal_out, embed_out):
    time_value = jnp.take(timesteps, levels).astype(jnp.float32)
    earlier = jnp.take(timesteps, levels - 1).astype(jnp.float32)
    step_size = (earlier - time_value) / 1000.0
    modulation = time_modulation(time_value, time_proj)
    pieces = jnp.split(modulation, 6, axis=-1)
    shift_s, scale_s, gate_s, shift_t, scale_t, gate_t = [piece[:, None, :] for piece in pieces]
    latent = latents
    outputs = []
    for step_index in range(STEPS):
        hidden_in = jnp.dot(latent.astype(jnp.bfloat16), embed_in, preferred_element_type=jnp.float32)
        normed = (layer_norm(hidden_in) * (1.0 + scale_s) + shift_s).astype(jnp.bfloat16)
        triple = jnp.dot(normed, spatial_proj, preferred_element_type=jnp.float32).astype(jnp.bfloat16)
        mixed = lax.map(spatial_frame, triple)
        hidden_spatial = hidden_in + gate_s * jnp.dot(mixed, spatial_out, preferred_element_type=jnp.float32)
        normed = (layer_norm(hidden_spatial) * (1.0 + scale_t) + shift_t).astype(jnp.bfloat16)
        triple = jnp.dot(normed, temporal_proj, preferred_element_type=jnp.float32).astype(jnp.bfloat16)
        mixed = temporal_attention(triple, window_offsets[step_index])
        hidden_temporal = hidden_spatial + gate_t * jnp.dot(mixed, temporal_out, preferred_element_type=jnp.float32)
        velocity = jnp.dot(layer_norm(hidden_temporal).astype(jnp.bfloat16), embed_out, preferred_element_type=jnp.float32)
        outputs.append(velocity)
        stepped = latent + step_size[:, None, None] * velocity
        if step_index + 1 < STEPS:
            latent = jnp.concatenate([stepped[1:], fresh_noise[step_index][None]], 0)
        else:
            latent = stepped
    return (latent, jnp.stack(outputs))
```

```python
import math

import jax
import jax.numpy as jnp
from jax import lax
from jax.sharding import PartitionSpec as P

HEADS = 16
HEAD = 72
WIN = 16
STEPS = 2
GROUPS = 4


epsilon = 1e-06


def layer_norm(values):
    center = values - jnp.mean(values, -1, keepdims=True)
    spread = jnp.mean(center * center, -1, keepdims=True)
    return center * lax.rsqrt(spread + epsilon)


def head_norm(values):
    wide = values.astype(jnp.float32)
    return (wide * lax.rsqrt(jnp.mean(wide * wide, -1, keepdims=True) + epsilon)).astype(
        jnp.bfloat16
    )


def lookup_table(indices, table):
    hits = indices[:, None] == jnp.arange(table.shape[0], dtype=jnp.int32)[None, :]
    return jnp.sum(jnp.where(hits, table[None, :], 0), axis=1).astype(jnp.float32)


def time_modulation(time_value, time_proj):
    half = time_proj.shape[0] // 2
    freqs = jnp.exp(-math.log(10000.0) * jnp.arange(half, dtype=jnp.float32) / half)
    angles = time_value[:, None] * freqs[None, :]
    features = jnp.concatenate([jnp.cos(angles), jnp.sin(angles)], -1).astype(jnp.bfloat16)
    return jnp.dot(features, time_proj, preferred_element_type=jnp.float32)


def softmax_rows(scores):
    raised = jnp.exp(scores)
    return (raised / jnp.sum(raised, -1, keepdims=True)).astype(jnp.bfloat16)


def spatial_block(tokens, embed_in, shift, scale, weights):
    hidden = jnp.dot(tokens, embed_in, preferred_element_type=jnp.float32)
    normed = (layer_norm(hidden) * (1.0 + scale) + shift).astype(jnp.bfloat16)
    triple = jnp.dot(normed, weights, preferred_element_type=jnp.float32).astype(jnp.bfloat16)
    split = triple.reshape(triple.shape[0], 3, HEADS // GROUPS, HEAD)
    queries = head_norm(split[:, 0])
    keys = head_norm(split[:, 1])
    scores = jnp.einsum(
        "qhd,khd->hqk", queries, keys, preferred_element_type=jnp.float32
    ) * HEAD ** (-0.5)
    weights = softmax_rows(scores)
    mixed = jnp.einsum("hqk,khd->qhd", weights, split[:, 2], preferred_element_type=jnp.float32)
    return mixed.astype(jnp.bfloat16).reshape(triple.shape[0], -1)


def temporal_block(mixed, latent, mods, offset, embed_in, spatial_out, proj, out, embed_out):
    gate_s, shift_t, scale_t, gate_t = [mod[:, None, :] for mod in mods]
    frames, tokens = mixed.shape[:2]
    hidden_in = jnp.dot(latent.astype(jnp.bfloat16), embed_in, preferred_element_type=jnp.float32)
    hidden = hidden_in + gate_s * jnp.dot(mixed, spatial_out, preferred_element_type=jnp.float32)
    normed = (layer_norm(hidden) * (1.0 + scale_t) + shift_t).astype(jnp.bfloat16)
    triple = jnp.dot(normed, proj, preferred_element_type=jnp.float32).astype(jnp.bfloat16)
    split = triple.reshape(frames, tokens, 3, HEADS, HEAD)
    queries = head_norm(split[:, :, 0])
    keys = head_norm(split[:, :, 1])
    window = (jnp.arange(frames, dtype=jnp.int32) + WIN - offset) // WIN
    same = window[:, None] == window[None, :]
    scores = jnp.einsum(
        "fthd,gthd->thfg", queries, keys, preferred_element_type=jnp.float32
    ) * HEAD ** (-0.5)
    weights = softmax_rows(jnp.where(same[None, None], scores, -1e30))
    mixed = jnp.einsum(
        "thfg,gthd->fthd", weights, split[:, :, 2], preferred_element_type=jnp.float32
    )
    mixed = mixed.astype(jnp.bfloat16).reshape(frames, tokens, HEADS * HEAD)
    hidden = hidden + gate_t * jnp.dot(mixed, out, preferred_element_type=jnp.float32)
    return jnp.dot(
        layer_norm(hidden).astype(jnp.bfloat16), embed_out, preferred_element_type=jnp.float32
    )


def to_tokens(values):
    return lax.all_to_all(values, "frame", split_axis=1, concat_axis=0, tiled=True)


def to_frames(values):
    return lax.all_to_all(values, "frame", split_axis=0, concat_axis=1, tiled=True)


def local(
    latents,
    fresh_noise,
    levels,
    timesteps,
    window_offsets,
    time_proj,
    embed_in,
    spatial_proj,
    spatial_out,
    temporal_proj,
    temporal_out,
    embed_out,
):
    place, row = lax.axis_index("space"), lax.axis_index("frame")
    which, group = place // GROUPS, place % GROUPS
    heads = spatial_proj.reshape(-1, 3, GROUPS, HEADS // GROUPS * HEAD)
    own = lax.dynamic_index_in_dim(heads, group, 2, keepdims=False)
    spatial_own = lax.all_gather(own.reshape(own.shape[0], -1), "frame", axis=0, tiled=True)
    spatial_back = lax.all_gather(spatial_out, "frame", axis=0, tiled=True)
    temporal_full = lax.all_gather(temporal_proj, "frame", axis=0, tiled=True)
    temporal_back = lax.all_gather(temporal_out, "frame", axis=0, tiled=True)
    all_levels = lax.all_gather(levels, "frame", axis=0, tiled=True)
    time_value = lookup_table(all_levels, timesteps)
    earlier = lookup_table(all_levels - 1, timesteps)
    step_size = (earlier - time_value) / 1000.0
    modulation = time_modulation(time_value, time_proj)
    shift_s, scale_s, gate_s, shift_t, scale_t, gate_t = jnp.split(modulation, 6, axis=-1)
    frame = row * latents.shape[0] + which
    shift_own = lax.dynamic_slice_in_dim(shift_s, frame, 1)
    scale_own = lax.dynamic_slice_in_dim(scale_s, frame, 1)
    latent = to_tokens(latents)
    fresh = lax.dynamic_slice_in_dim(fresh_noise, row * latent.shape[1], latent.shape[1], 1)
    by_frame = latents.astype(jnp.bfloat16)
    outputs = []
    for step_index in range(STEPS):
        whole = lax.all_gather(by_frame, "space", axis=1, tiled=True)
        tokens = lax.dynamic_index_in_dim(whole, which, 0, keepdims=False)
        mixed = spatial_block(tokens, embed_in, shift_own, scale_own, spatial_own)
        parts = mixed.reshape(8, -1, mixed.shape[-1])
        parts = lax.all_to_all(parts, "space", split_axis=0, concat_axis=0)
        parts = parts.reshape(2, GROUPS, parts.shape[1], -1)
        parts = jnp.moveaxis(parts, 1, 2).reshape(2, parts.shape[2], -1)
        velocity = temporal_block(
            to_tokens(parts),
            latent,
            (gate_s, shift_t, scale_t, gate_t),
            window_offsets[step_index],
            embed_in,
            spatial_back,
            temporal_full,
            temporal_back,
            embed_out,
        )
        outputs.append(velocity)
        stepped = latent + step_size[:, None, None] * velocity
        if step_index + 1 < STEPS:
            latent = jnp.concatenate([stepped[1:], fresh[step_index][None]], 0)
            by_frame = to_frames(latent.astype(jnp.bfloat16))
        else:
            latent = stepped
    result = to_frames(jnp.concatenate([latent] + outputs, -1))
    size = latent.shape[-1]
    queue = result[..., :size]
    return (queue, jnp.stack([result[..., size : 2 * size], result[..., 2 * size :]]))


def solution(mesh):
    return jax.shard_map(
        local,
        mesh=mesh,
        in_specs=(
            P("frame", "space", None),
            P(None, "space", None),
            P("frame"),
            P(),
            P(),
            P(),
            P(),
            P("frame", None),
            P("frame", None),
            P("frame", None),
            P("frame", None),
            P(),
        ),
        out_specs=(P("frame", "space", None), P(None, "frame", "space", None)),
        check_vma=False,
    )
```

```python
import math

import jax
import jax.numpy as jnp
from jax import lax
from jax.experimental import pallas as pl
from jax.experimental.pallas import tpu as pltpu
from jax.sharding import PartitionSpec as P

HEADS = 16
HEAD = 72
WIN = 16
STEPS = 2
GROUPS = 4
LANES = 128
SUB = 8
BLOCK = 256
SHARPEN = HEAD ** (-0.5) * math.log2(math.e)
VMEM_BYTES = 56 * 2**20


epsilon = 1e-06


def layer_norm(values):
    center = values - jnp.mean(values, -1, keepdims=True)
    spread = jnp.mean(center * center, -1, keepdims=True)
    return center * lax.rsqrt(spread + epsilon)


def lookup_table(indices, table):
    hits = indices[:, None] == jnp.arange(table.shape[0], dtype=jnp.int32)[None, :]
    return jnp.sum(jnp.where(hits, table[None, :], 0), axis=1).astype(jnp.float32)


def time_modulation(time_value, time_proj):
    half = time_proj.shape[0] // 2
    freqs = jnp.exp(-math.log(10000.0) * jnp.arange(half, dtype=jnp.float32) / half)
    angles = time_value[:, None] * freqs[None, :]
    features = jnp.concatenate([jnp.cos(angles), jnp.sin(angles)], -1).astype(jnp.bfloat16)
    return jnp.dot(features, time_proj, preferred_element_type=jnp.float32)


def head_scale(values):
    return lax.rsqrt(jnp.mean(values * values, -1, keepdims=True) + epsilon)


def one_column(rows):
    lane = lax.broadcasted_iota(jnp.int32, (rows, LANES - HEAD), 1)
    return jnp.where(lane == 0, 1.0, 0.0).astype(jnp.bfloat16)


def contract_last(left, right):
    return lax.dot_general(
        left, right, (((1,), (1,)), ((), ())), preferred_element_type=jnp.float32
    )


def spatial_kernel(tokens, embed, shift, scale, weights, out, triple, qs, ks, vs):
    rows, local_heads = tokens.shape[0], HEADS // GROUPS
    for first in range(0, rows, BLOCK):
        here = pl.ds(first, BLOCK)
        hidden = jnp.dot(tokens[here, :], embed[...], preferred_element_type=jnp.float32)
        normed = layer_norm(hidden) * (1.0 + scale[...]) + shift[...]
        triple[...] = jnp.dot(
            normed.astype(jnp.bfloat16), weights[...], preferred_element_type=jnp.float32
        )
        for head in range(local_heads):
            query = triple[:, head * HEAD : (head + 1) * HEAD]
            key = triple[:, (local_heads + head) * HEAD : (local_heads + head + 1) * HEAD]
            value = triple[:, (2 * local_heads + head) * HEAD : (2 * local_heads + head + 1) * HEAD]
            qs[head, here, :] = (query * (head_scale(query) * SHARPEN)).astype(jnp.bfloat16)
            ks[head, here, :] = (key * head_scale(key)).astype(jnp.bfloat16)
            vs[head, here, :HEAD] = value.astype(jnp.bfloat16)
            vs[head, here, HEAD:] = one_column(BLOCK)
    for first in range(0, rows, BLOCK):
        here = pl.ds(first, BLOCK)
        for head in range(local_heads):
            raised = jnp.exp2(contract_last(qs[head, here, :], ks[head])).astype(jnp.bfloat16)
            mix = jnp.dot(raised, vs[head], preferred_element_type=jnp.float32)
            mix = mix[:, :HEAD] / mix[:, HEAD : HEAD + 1]
            out[here, head * HEAD : (head + 1) * HEAD] = mix.astype(jnp.bfloat16)


def spatial_block(tokens, embed_in, shift, scale, weights):
    rows, local_heads = tokens.shape[0], HEADS // GROUPS
    return pl.pallas_call(
        spatial_kernel,
        out_shape=jax.ShapeDtypeStruct((rows, local_heads * HEAD), jnp.bfloat16),
        in_specs=[pl.BlockSpec(memory_space=pltpu.VMEM)] * 5,
        out_specs=pl.BlockSpec(memory_space=pltpu.VMEM),
        scratch_shapes=[
            pltpu.VMEM((BLOCK, 3 * local_heads * HEAD), jnp.float32),
            pltpu.VMEM((local_heads, rows, HEAD), jnp.bfloat16),
            pltpu.VMEM((local_heads, rows, HEAD), jnp.bfloat16),
            pltpu.VMEM((local_heads, rows, LANES), jnp.bfloat16),
        ],
        compiler_params=pltpu.CompilerParams(vmem_limit_bytes=VMEM_BYTES),
        name="spatial",
    )(tokens, embed_in, shift, scale, weights)


def temporal_kernel(
    offset, mixed, latent, gate_s, shift_t, scale_t, gate_t,
    embed_in, spatial_out, proj, out, embed_out, velocity, triple, mix,
):
    rows, frames = mixed.shape[0], gate_s.shape[0]
    tokens = rows // frames
    width = HEADS * HEAD

    def spread(mod):
        wide = jnp.broadcast_to(
            mod.reshape(frames // SUB, 1, SUB, width), (frames // SUB, tokens, SUB, width)
        )
        return wide.reshape(rows, width)

    hidden_in = jnp.dot(
        latent[...].astype(jnp.bfloat16), embed_in[...], preferred_element_type=jnp.float32
    )
    back = jnp.dot(mixed[...], spatial_out[...], preferred_element_type=jnp.float32)
    hidden = hidden_in + spread(gate_s[...]) * back
    normed = layer_norm(hidden) * (1.0 + spread(scale_t[...])) + spread(shift_t[...])
    triple[...] = jnp.dot(
        normed.astype(jnp.bfloat16), proj[...], preferred_element_type=jnp.float32
    )

    def place(index):
        block, rest = index // (tokens * SUB), index % (tokens * SUB)
        frame = block * SUB + rest % SUB
        return (frame + WIN - offset[0]) // WIN, rest // SUB

    window_row, token_row = place(lax.broadcasted_iota(jnp.int32, (rows, rows), 0))
    window_col, token_col = place(lax.broadcasted_iota(jnp.int32, (rows, rows), 1))
    same = (window_row == window_col) & (token_row == token_col)
    ones = one_column(rows)
    for head in range(HEADS):
        query = triple[:, head * HEAD : (head + 1) * HEAD]
        key = triple[:, width + head * HEAD : width + (head + 1) * HEAD]
        value = triple[:, 2 * width + head * HEAD : 2 * width + (head + 1) * HEAD]
        query = (query * (head_scale(query) * SHARPEN)).astype(jnp.bfloat16)
        key = (key * head_scale(key)).astype(jnp.bfloat16)
        value = jnp.concatenate([value.astype(jnp.bfloat16), ones], -1)
        raised = jnp.where(same, jnp.exp2(contract_last(query, key)), 0.0).astype(jnp.bfloat16)
        part = jnp.dot(raised, value, preferred_element_type=jnp.float32)
        part = part[:, :HEAD] / part[:, HEAD : HEAD + 1]
        mix[:, head * HEAD : (head + 1) * HEAD] = part.astype(jnp.bfloat16)
    forth = jnp.dot(mix[...], out[...], preferred_element_type=jnp.float32)
    hidden = hidden + spread(gate_t[...]) * forth
    velocity[...] = jnp.dot(
        layer_norm(hidden).astype(jnp.bfloat16), embed_out[...], preferred_element_type=jnp.float32
    )


def temporal_block(mixed, latent, mods, offset, embed_in, spatial_out, proj, out, embed_out):
    frames, tokens = mixed.shape[:2]

    def fold(value):
        parts = value.reshape(frames // SUB, SUB, tokens, -1)
        return jnp.moveaxis(parts, 1, 2).reshape(frames * tokens, -1)

    velocity = pl.pallas_call(
        temporal_kernel,
        out_shape=jax.ShapeDtypeStruct((frames * tokens, latent.shape[-1]), jnp.float32),
        in_specs=[pl.BlockSpec(memory_space=pltpu.SMEM)]
        + [pl.BlockSpec(memory_space=pltpu.VMEM)] * 11,
        out_specs=pl.BlockSpec(memory_space=pltpu.VMEM),
        scratch_shapes=[
            pltpu.VMEM((frames * tokens, 3 * HEADS * HEAD), jnp.float32),
            pltpu.VMEM((frames * tokens, HEADS * HEAD), jnp.bfloat16),
        ],
        compiler_params=pltpu.CompilerParams(vmem_limit_bytes=VMEM_BYTES),
        name="temporal",
    )(
        offset[None], fold(mixed), fold(latent), *mods,
        embed_in, spatial_out, proj, out, embed_out,
    )
    velocity = velocity.reshape(frames // SUB, tokens, SUB, -1)
    return jnp.moveaxis(velocity, 1, 2).reshape(frames, tokens, -1)


def to_tokens(values):
    return lax.all_to_all(values, "frame", split_axis=1, concat_axis=0, tiled=True)


def to_frames(values):
    return lax.all_to_all(values, "frame", split_axis=0, concat_axis=1, tiled=True)


def local(
    latents,
    fresh_noise,
    levels,
    timesteps,
    window_offsets,
    time_proj,
    embed_in,
    spatial_proj,
    spatial_out,
    temporal_proj,
    temporal_out,
    embed_out,
):
    place, row = lax.axis_index("space"), lax.axis_index("frame")
    which, group = place // GROUPS, place % GROUPS
    heads = spatial_proj.reshape(-1, 3, GROUPS, HEADS // GROUPS * HEAD)
    own = lax.dynamic_index_in_dim(heads, group, 2, keepdims=False)
    spatial_own = lax.all_gather(own.reshape(own.shape[0], -1), "frame", axis=0, tiled=True)
    spatial_back = lax.all_gather(spatial_out, "frame", axis=0, tiled=True)
    temporal_full = lax.all_gather(temporal_proj, "frame", axis=0, tiled=True)
    temporal_back = lax.all_gather(temporal_out, "frame", axis=0, tiled=True)
    all_levels = lax.all_gather(levels, "frame", axis=0, tiled=True)
    time_value = lookup_table(all_levels, timesteps)
    earlier = lookup_table(all_levels - 1, timesteps)
    step_size = (earlier - time_value) / 1000.0
    modulation = time_modulation(time_value, time_proj)
    shift_s, scale_s, gate_s, shift_t, scale_t, gate_t = jnp.split(modulation, 6, axis=-1)
    frame = row * latents.shape[0] + which
    shift_own = lax.dynamic_slice_in_dim(shift_s, frame, 1)
    scale_own = lax.dynamic_slice_in_dim(scale_s, frame, 1)
    latent = to_tokens(latents)
    fresh = lax.dynamic_slice_in_dim(fresh_noise, row * latent.shape[1], latent.shape[1], 1)
    by_frame = latents.astype(jnp.bfloat16)
    outputs = []
    for step_index in range(STEPS):
        whole = lax.all_gather(by_frame, "space", axis=1, tiled=True)
        tokens = lax.dynamic_index_in_dim(whole, which, 0, keepdims=False)
        mixed = spatial_block(tokens, embed_in, shift_own, scale_own, spatial_own)
        parts = mixed.reshape(8, -1, mixed.shape[-1])
        parts = lax.all_to_all(parts, "space", split_axis=0, concat_axis=0)
        parts = parts.reshape(2, GROUPS, parts.shape[1], -1)
        parts = jnp.moveaxis(parts, 1, 2).reshape(2, parts.shape[2], -1)
        velocity = temporal_block(
            to_tokens(parts),
            latent,
            (gate_s, shift_t, scale_t, gate_t),
            window_offsets[step_index],
            embed_in,
            spatial_back,
            temporal_full,
            temporal_back,
            embed_out,
        )
        outputs.append(velocity)
        stepped = latent + step_size[:, None, None] * velocity
        if step_index + 1 < STEPS:
            latent = jnp.concatenate([stepped[1:], fresh[step_index][None]], 0)
            by_frame = to_frames(latent.astype(jnp.bfloat16))
        else:
            latent = stepped
    result = to_frames(jnp.concatenate([latent] + outputs, -1))
    size = latent.shape[-1]
    queue = result[..., :size]
    return (queue, jnp.stack([result[..., size : 2 * size], result[..., 2 * size :]]))


def solution(mesh):
    return jax.shard_map(
        local,
        mesh=mesh,
        in_specs=(
            P("frame", "space", None),
            P(None, "space", None),
            P("frame"),
            P(),
            P(),
            P(),
            P(),
            P("frame", None),
            P("frame", None),
            P("frame", None),
            P("frame", None),
            P(),
        ),
        out_specs=(P("frame", "space", None), P(None, "frame", "space", None)),
        check_vma=False,
    )
```

```python
import math

import jax
import jax.numpy as jnp
from jax import lax
from jax.experimental import pallas as pl
from jax.experimental.pallas import tpu as pltpu
from jax.sharding import PartitionSpec as P

HEADS = 16
HEAD = 72
WIN = 16
STEPS = 2
GROUPS = 4
LANES = 128
SUB = 8
TILE = 16
TOP = 32
MESH = pl.DeviceIdType.MESH
BLOCK = 256
SHARPEN = HEAD ** (-0.5) * math.log2(math.e)
VMEM_BYTES = 56 * 2**20


epsilon = 1e-06


def layer_norm(values):
    center = values - jnp.mean(values, -1, keepdims=True)
    spread = jnp.mean(center * center, -1, keepdims=True)
    return center * lax.rsqrt(spread + epsilon)


def lookup_table(indices, table):
    hits = indices[:, None] == jnp.arange(table.shape[0], dtype=jnp.int32)[None, :]
    return jnp.sum(jnp.where(hits, table[None, :], 0), axis=1).astype(jnp.float32)


def time_modulation(time_value, time_proj):
    half = time_proj.shape[0] // 2
    freqs = jnp.exp(-math.log(10000.0) * jnp.arange(half, dtype=jnp.float32) / half)
    angles = time_value[:, None] * freqs[None, :]
    features = jnp.concatenate([jnp.cos(angles), jnp.sin(angles)], -1).astype(jnp.bfloat16)
    return jnp.dot(features, time_proj, preferred_element_type=jnp.float32)


def sites():
    frame, space = lax.axis_index("frame"), lax.axis_index("space")
    return frame // 16, frame // 2 % 8, frame % 2, space // 2, space % 2


def site_id(high, z, core, y, low):
    return {"frame": high * 16 + z * 2 + core, "space": y * 2 + low}


def meet(peers):
    barrier = pltpu.get_barrier_semaphore()
    for peer in peers:
        pl.semaphore_signal(barrier, inc=1, device_id=peer, device_id_type=MESH)
    pl.semaphore_wait(barrier, len(peers))


def gather_kernel(
    proj_s, out_s, proj_t, out_t, own_out, rest_out,
    own_main, own_rest, main, rest, tail_s, tail_t, send_sem, recv_sem,
):
    high, z, core, y, low = sites()
    up = site_id(high, (z + 1) % 8, core, y, low)
    down = site_id(high, (z + 7) % 8, core, y, low)
    across = site_id(1 - high, z, core, y, 1 - low)
    north = site_id(high, z, core, (y + 1) % 4, low)
    south = site_id(high, z, core, (y + 3) % 4, low)
    sibling = site_id(high, z, 1 - core, y, low)
    meet([up, down, across, north, south, sibling])

    def slot(half, level):
        return half * 16 + (level % 8) * 2 + core

    mine = slot(high, z)
    group = y
    span = HEADS // GROUPS * HEAD
    width = HEADS * HEAD
    source = lax.broadcasted_iota(jnp.int32, (width, span), 0)
    target = lax.broadcasted_iota(jnp.int32, (width, span), 1)
    chosen = jnp.where(source == target + group * span, 1.0, 0.0).astype(jnp.bfloat16)
    here = pl.ds(pl.multiple_of(mine * TOP, TOP), TOP)
    for part in range(3):
        piece = jnp.dot(
            proj_s[:, part * width : (part + 1) * width], chosen, preferred_element_type=jnp.float32
        )
        own_main[here, part * span : (part + 1) * span] = piece[:TOP].astype(jnp.bfloat16)
        tail_s[0:4, part * span : (part + 1) * span] = piece[TOP:]
    own_main[here, 3 * span :] = jnp.zeros((TOP, own_main.shape[1] - 3 * span), jnp.bfloat16)
    tail_s[0:4, 3 * span :] = jnp.zeros((4, tail_s.shape[1] - 3 * span), jnp.float32)
    first = 0
    for piece in (out_s, proj_t, out_t):
        columns = pl.ds(first, piece.shape[1])
        main[here, columns] = piece[:TOP, :]
        tail_t[0:4, columns] = piece[TOP:, :].astype(jnp.float32)
        first += piece.shape[1]
    tail_t[0:4, first:] = jnp.zeros((4, tail_t.shape[1] - first), jnp.float32)
    below = pl.ds(pl.multiple_of(mine * TILE, TILE), TILE)
    for packed, tail in ((own_rest, tail_s), (rest, tail_t)):
        size = packed.shape[1]
        quarters = [tail[0:4, a * size : (a + 1) * size] for a in range(4)]
        packed[below, :] = jnp.concatenate(quarters, 0).astype(jnp.bfloat16)

    arrays = ((own_main, TOP), (own_rest, TILE), (main, TOP), (rest, TILE))
    started = []

    def copies(kind, which, peer, index, half=None):
        made = []
        for number in (2 * kind, 2 * kind + 1):
            array, rows = arrays[number]
            first, count = which * rows, rows
            if half is not None:
                if rows == TOP:
                    first, count = first + half * TILE, TILE
                elif half == 1:
                    continue
            piece = array.at[pl.ds(pl.multiple_of(first, TILE), count), :]
            made.append(
                pltpu.make_async_remote_copy(
                    src_ref=piece,
                    dst_ref=piece,
                    send_sem=send_sem.at[index, number],
                    recv_sem=recv_sem.at[index, number],
                    device_id=peer,
                    device_id_type=MESH,
                )
            )
        return made

    def send(kind, which, peer, index, half=None):
        for copy in copies(kind, which, peer, index, half):
            copy.start()
            started.append(copy)

    def arrive(kind, which, peer, index, half=None):
        for copy in copies(kind, which, peer, index, half):
            copy.wait_recv()

    HANDED, ACROSS = 16, 32
    handed = ([], [])

    def hand(kind, which):
        send(kind, which, sibling, HANDED + len(handed[kind]))
        handed[kind].append(which)

    def ring(kind, reach):
        for hop in range(1, 5):
            half = (0, 1) if hop == 4 else (None, None)
            lower, upper = slot(high, z + 8 - hop), slot(high, z + hop)
            arrive(kind, lower, up, hop - 1, half[0])
            if hop < 4:
                send(kind, lower, up, hop, 0 if hop == 3 else None)
            arrive(kind, upper, down, 4 + hop - 1, half[1])
            if hop < 4:
                send(kind, upper, down, 4 + hop, 1 if hop == 3 else None)
                hand(kind, lower)
                reach(hop, lower)
            hand(kind, upper)
            reach(hop, upper)

    for kind in (0, 1):
        send(kind, mine, up, 0)
        send(kind, mine, down, 4)
        hand(kind, mine)
        if kind == 0:
            send(kind, mine, across, ACROSS)

    passed = [mine]

    def pass_across(hop, which):
        send(0, which, across, ACROSS + len(passed))
        passed.append(which)

    ring(0, pass_across)
    for index, which in enumerate(passed):
        other = which + 16 - 32 * high
        arrive(0, other, across, ACROSS + index)
        hand(0, other)

    def two_across(hop, which):
        if hop == 2 and len(handed[1]) == 5:
            send(1, slot(high, z + y + 7), across, 8)
        if hop == 4:
            send(1, slot(high, z + y + 3), across, 9)

    ring(1, two_across)
    near, far = slot(1 - high, z + y + 7), slot(1 - high, z + y + 3)
    before, after, opposite = (y + 3) % 4, (y + 1) % 4, (y + 2) % 4
    for which, index in ((near, 0), (far, 1)):
        arrive(1, which, across, 8 + index)
        send(1, which, north, 10 + index)
        send(1, which, south, 12 + index)
        hand(1, which)
    steps = (
        (before, 7, north, 10, 14),
        (after, 7, south, 12, None),
        (after, 3, south, 13, 15),
        (before, 3, north, 11, None),
        (opposite, 7, north, 14, None),
        (opposite, 3, south, 15, None),
    )
    for place, shift, way, index, onward in steps:
        which = slot(1 - high, z + place + shift)
        arrive(1, which, way, index)
        if onward is not None:
            send(1, which, way, onward)
        hand(1, which)
    for kind in (0, 1):
        for index, which in enumerate(handed[kind]):
            arrive(kind, which + 1 - 2 * core, sibling, HANDED + index)
    for copy in started:
        copy.wait_send()

    for top, low_rows, whole in ((own_main, own_rest, own_out), (main, rest, rest_out)):
        size = low_rows.shape[1]
        for quarter in range(4):
            lo, hi = quarter * size, min((quarter + 1) * size, whole.shape[1])
            order = restore_order(quarter)

            @pl.loop(0, 8)
            def _(quad):
                pieces = jnp.concatenate(
                    [
                        top[pl.ds(pl.multiple_of(quad * 4 * TOP, 4 * TOP), 4 * TOP), lo:hi],
                        low_rows[pl.ds(pl.multiple_of(quad * 4 * TILE, 4 * TILE), 4 * TILE), : hi - lo],
                    ],
                    0,
                )
                rows = jnp.dot(order, pieces, preferred_element_type=jnp.float32)
                whole[pl.ds(pl.multiple_of(quad * 144, 16), 144), lo:hi] = rows.astype(jnp.bfloat16)


def restore_order(quarter):
    row = lax.broadcasted_iota(jnp.int32, (144, 4 * TOP + 4 * TILE), 0)
    column = lax.broadcasted_iota(jnp.int32, (144, 4 * TOP + 4 * TILE), 1)
    device, inner = row // 36, row % 36
    source = jnp.where(
        inner < TOP, device * TOP + inner, 4 * TOP + device * TILE + quarter * 4 + inner - TOP
    )
    return jnp.where(source == column, 1.0, 0.0).astype(jnp.bfloat16)


def gather_weights(spatial_proj, spatial_out, temporal_proj, temporal_out):
    width = HEADS * HEAD
    own, other = 7 * LANES, 5 * width
    packed = (2 * LANES, 12 * LANES)
    return pl.pallas_call(
        gather_kernel,
        out_shape=[
            jax.ShapeDtypeStruct((width, own), jnp.bfloat16),
            jax.ShapeDtypeStruct((width, other), jnp.bfloat16),
        ],
        in_specs=[pl.BlockSpec(memory_space=pltpu.VMEM)] * 4,
        out_specs=[pl.BlockSpec(memory_space=pltpu.VMEM)] * 2,
        scratch_shapes=[
            pltpu.VMEM((32 * TOP, own), jnp.bfloat16),
            pltpu.VMEM((32 * TILE, packed[0]), jnp.bfloat16),
            pltpu.VMEM((32 * TOP, other), jnp.bfloat16),
            pltpu.VMEM((32 * TILE, packed[1]), jnp.bfloat16),
            pltpu.VMEM((SUB, 4 * packed[0]), jnp.float32),
            pltpu.VMEM((SUB, 4 * packed[1]), jnp.float32),
            pltpu.SemaphoreType.DMA((40, 4)),
            pltpu.SemaphoreType.DMA((40, 4)),
        ],
        compiler_params=pltpu.CompilerParams(
            collective_id=0, has_side_effects=True, vmem_limit_bytes=VMEM_BYTES
        ),
        name="gather",
    )(spatial_proj, spatial_out, temporal_proj, temporal_out)


def head_scale(values):
    return lax.rsqrt(jnp.mean(values * values, -1, keepdims=True) + epsilon)


def one_column(rows):
    lane = lax.broadcasted_iota(jnp.int32, (rows, LANES - HEAD), 1)
    return jnp.where(lane == 0, 1.0, 0.0).astype(jnp.bfloat16)


def contract_last(left, right):
    return lax.dot_general(
        left, right, (((1,), (1,)), ((), ())), preferred_element_type=jnp.float32
    )


def spatial_kernel(tokens, embed, shift, scale, weights, out, triple, qs, ks, vs):
    rows, local_heads = tokens.shape[0], HEADS // GROUPS
    for first in range(0, rows, BLOCK):
        here = pl.ds(first, BLOCK)
        hidden = jnp.dot(tokens[here, :], embed[...], preferred_element_type=jnp.float32)
        normed = layer_norm(hidden) * (1.0 + scale[...]) + shift[...]
        triple[...] = jnp.dot(
            normed.astype(jnp.bfloat16), weights[...], preferred_element_type=jnp.float32
        )
        for head in range(local_heads):
            query = triple[:, head * HEAD : (head + 1) * HEAD]
            key = triple[:, (local_heads + head) * HEAD : (local_heads + head + 1) * HEAD]
            value = triple[:, (2 * local_heads + head) * HEAD : (2 * local_heads + head + 1) * HEAD]
            qs[head, here, :] = (query * (head_scale(query) * SHARPEN)).astype(jnp.bfloat16)
            ks[head, here, :] = (key * head_scale(key)).astype(jnp.bfloat16)
            vs[head, here, :HEAD] = value.astype(jnp.bfloat16)
            vs[head, here, HEAD:] = one_column(BLOCK)
    for first in range(0, rows, BLOCK):
        here = pl.ds(first, BLOCK)
        for head in range(local_heads):
            raised = jnp.exp2(contract_last(qs[head, here, :], ks[head])).astype(jnp.bfloat16)
            mix = jnp.dot(raised, vs[head], preferred_element_type=jnp.float32)
            mix = mix[:, :HEAD] / mix[:, HEAD : HEAD + 1]
            out[here, head * HEAD : (head + 1) * HEAD] = mix.astype(jnp.bfloat16)


def spatial_block(tokens, embed_in, shift, scale, weights):
    rows, local_heads = tokens.shape[0], HEADS // GROUPS
    return pl.pallas_call(
        spatial_kernel,
        out_shape=jax.ShapeDtypeStruct((rows, local_heads * HEAD), jnp.bfloat16),
        in_specs=[pl.BlockSpec(memory_space=pltpu.VMEM)] * 5,
        out_specs=pl.BlockSpec(memory_space=pltpu.VMEM),
        scratch_shapes=[
            pltpu.VMEM((BLOCK, weights.shape[1]), jnp.float32),
            pltpu.VMEM((local_heads, rows, HEAD), jnp.bfloat16),
            pltpu.VMEM((local_heads, rows, HEAD), jnp.bfloat16),
            pltpu.VMEM((local_heads, rows, LANES), jnp.bfloat16),
        ],
        compiler_params=pltpu.CompilerParams(vmem_limit_bytes=VMEM_BYTES),
        name="spatial",
    )(tokens, embed_in, shift, scale, weights)


def temporal_kernel(
    offset, mixed, latent, gate_s, shift_t, scale_t, gate_t,
    embed_in, shared, embed_out, velocity, triple, mix,
):
    rows, frames = mixed.shape[0], gate_s.shape[0]
    tokens = rows // frames
    width = HEADS * HEAD

    def spread(mod):
        wide = jnp.broadcast_to(
            mod.reshape(frames // SUB, 1, SUB, width), (frames // SUB, tokens, SUB, width)
        )
        return wide.reshape(rows, width)

    hidden_in = jnp.dot(
        latent[...].astype(jnp.bfloat16), embed_in[...], preferred_element_type=jnp.float32
    )
    back = jnp.dot(mixed[...], shared[:, :width], preferred_element_type=jnp.float32)
    hidden = hidden_in + spread(gate_s[...]) * back
    normed = layer_norm(hidden) * (1.0 + spread(scale_t[...])) + spread(shift_t[...])
    triple[...] = jnp.dot(
        normed.astype(jnp.bfloat16), shared[:, width : 4 * width], preferred_element_type=jnp.float32
    )

    def place(index):
        block, rest = index // (tokens * SUB), index % (tokens * SUB)
        frame = block * SUB + rest % SUB
        return (frame + WIN - offset[0]) // WIN, rest // SUB

    window_row, token_row = place(lax.broadcasted_iota(jnp.int32, (rows, rows), 0))
    window_col, token_col = place(lax.broadcasted_iota(jnp.int32, (rows, rows), 1))
    same = (window_row == window_col) & (token_row == token_col)
    ones = one_column(rows)
    for head in range(HEADS):
        query = triple[:, head * HEAD : (head + 1) * HEAD]
        key = triple[:, width + head * HEAD : width + (head + 1) * HEAD]
        value = triple[:, 2 * width + head * HEAD : 2 * width + (head + 1) * HEAD]
        query = (query * (head_scale(query) * SHARPEN)).astype(jnp.bfloat16)
        key = (key * head_scale(key)).astype(jnp.bfloat16)
        value = jnp.concatenate([value.astype(jnp.bfloat16), ones], -1)
        raised = jnp.where(same, jnp.exp2(contract_last(query, key)), 0.0).astype(jnp.bfloat16)
        part = jnp.dot(raised, value, preferred_element_type=jnp.float32)
        part = part[:, :HEAD] / part[:, HEAD : HEAD + 1]
        mix[:, head * HEAD : (head + 1) * HEAD] = part.astype(jnp.bfloat16)
    forth = jnp.dot(mix[...], shared[:, 4 * width :], preferred_element_type=jnp.float32)
    hidden = hidden + spread(gate_t[...]) * forth
    velocity[...] = jnp.dot(
        layer_norm(hidden).astype(jnp.bfloat16), embed_out[...], preferred_element_type=jnp.float32
    )


def temporal_block(mixed, latent, mods, offset, embed_in, shared, embed_out):
    frames, tokens = mixed.shape[:2]

    def fold(value):
        parts = value.reshape(frames // SUB, SUB, tokens, -1)
        return jnp.moveaxis(parts, 1, 2).reshape(frames * tokens, -1)

    velocity = pl.pallas_call(
        temporal_kernel,
        out_shape=jax.ShapeDtypeStruct((frames * tokens, latent.shape[-1]), jnp.float32),
        in_specs=[pl.BlockSpec(memory_space=pltpu.SMEM)]
        + [pl.BlockSpec(memory_space=pltpu.VMEM)] * 9,
        out_specs=pl.BlockSpec(memory_space=pltpu.VMEM),
        scratch_shapes=[
            pltpu.VMEM((frames * tokens, 3 * HEADS * HEAD), jnp.float32),
            pltpu.VMEM((frames * tokens, HEADS * HEAD), jnp.bfloat16),
        ],
        compiler_params=pltpu.CompilerParams(vmem_limit_bytes=VMEM_BYTES),
        name="temporal",
    )(
        offset[None], fold(mixed), fold(latent), *mods,
        embed_in, shared, embed_out,
    )
    velocity = velocity.reshape(frames // SUB, tokens, SUB, -1)
    return jnp.moveaxis(velocity, 1, 2).reshape(frames, tokens, -1)


def to_tokens(values):
    return lax.all_to_all(values, "frame", split_axis=1, concat_axis=0, tiled=True)


def to_frames(values):
    return lax.all_to_all(values, "frame", split_axis=0, concat_axis=1, tiled=True)


def local(
    latents,
    fresh_noise,
    levels,
    timesteps,
    window_offsets,
    time_proj,
    embed_in,
    spatial_proj,
    spatial_out,
    temporal_proj,
    temporal_out,
    embed_out,
):
    place, row = lax.axis_index("space"), lax.axis_index("frame")
    which = place % 2
    spatial_own, shared = gather_weights(spatial_proj, spatial_out, temporal_proj, temporal_out)
    all_levels = lax.all_gather(levels, "frame", axis=0, tiled=True)
    time_value = lookup_table(all_levels, timesteps)
    earlier = lookup_table(all_levels - 1, timesteps)
    step_size = (earlier - time_value) / 1000.0
    modulation = time_modulation(time_value, time_proj)
    shift_s, scale_s, gate_s, shift_t, scale_t, gate_t = jnp.split(modulation, 6, axis=-1)
    frame = row * latents.shape[0] + which
    shift_own = lax.dynamic_slice_in_dim(shift_s, frame, 1)
    scale_own = lax.dynamic_slice_in_dim(scale_s, frame, 1)
    latent = to_tokens(latents)
    fresh = lax.dynamic_slice_in_dim(fresh_noise, row * latent.shape[1], latent.shape[1], 1)
    by_frame = latents.astype(jnp.bfloat16)
    outputs = []
    for step_index in range(STEPS):
        whole = lax.all_gather(by_frame, "space", axis=1, tiled=True)
        tokens = lax.dynamic_index_in_dim(whole, which, 0, keepdims=False)
        mixed = spatial_block(tokens, embed_in, shift_own, scale_own, spatial_own)
        parts = mixed.reshape(8, -1, mixed.shape[-1])
        parts = lax.all_to_all(parts, "space", split_axis=0, concat_axis=0)
        parts = parts.reshape(GROUPS, 2, parts.shape[1], -1)
        parts = jnp.transpose(parts, (1, 2, 0, 3)).reshape(2, parts.shape[2], -1)
        velocity = temporal_block(
            to_tokens(parts),
            latent,
            (gate_s, shift_t, scale_t, gate_t),
            window_offsets[step_index],
            embed_in,
            shared,
            embed_out,
        )
        outputs.append(velocity)
        stepped = latent + step_size[:, None, None] * velocity
        if step_index + 1 < STEPS:
            latent = jnp.concatenate([stepped[1:], fresh[step_index][None]], 0)
            by_frame = to_frames(latent.astype(jnp.bfloat16))
        else:
            latent = stepped
    result = to_frames(jnp.concatenate([latent] + outputs, -1))
    size = latent.shape[-1]
    queue = result[..., :size]
    return (queue, jnp.stack([result[..., size : 2 * size], result[..., 2 * size :]]))


def solution(mesh):
    return jax.shard_map(
        local,
        mesh=mesh,
        in_specs=(
            P("frame", "space", None),
            P(None, "space", None),
            P("frame"),
            P(),
            P(),
            P(),
            P(),
            P("frame", None),
            P("frame", None),
            P("frame", None),
            P("frame", None),
            P(),
        ),
        out_specs=(P("frame", "space", None), P(None, "frame", "space", None)),
        check_vma=False,
    )
```

```python
import functools
import math

import jax
import jax.numpy as jnp
from jax import lax
from jax.experimental import pallas as pl
from jax.experimental.pallas import tpu as pltpu
from jax.sharding import PartitionSpec as P

HEADS = 16
HEAD = 72
WIN = 16
STEPS = 2
PATCH = 16
GROUPS = 4
LANES = 128
SUB = 8
TILE = 16
TOP = 32
MESH = pl.DeviceIdType.MESH
BLOCK = 256
SHARPEN = HEAD ** (-0.5) * math.log2(math.e)
VMEM_BYTES = 56 * 2**20


epsilon = 1e-06


def layer_norm(values):
    center = values - jnp.mean(values, -1, keepdims=True)
    spread = jnp.mean(center * center, -1, keepdims=True)
    return center * lax.rsqrt(spread + epsilon)


def lookup_table(indices, table):
    hits = indices[:, None] == jnp.arange(table.shape[0], dtype=jnp.int32)[None, :]
    return jnp.sum(jnp.where(hits, table[None, :], 0), axis=1).astype(jnp.float32)


def time_features(time_value, half):
    freqs = jnp.exp(-math.log(10000.0) * jnp.arange(half, dtype=jnp.float32) / half)
    angles = time_value[:, None] * freqs[None, :]
    return jnp.concatenate([jnp.cos(angles), jnp.sin(angles)], -1).astype(jnp.bfloat16)


def sites():
    frame, space = lax.axis_index("frame"), lax.axis_index("space")
    return frame // 16, frame // 2 % 8, frame % 2, space // 2, space % 2


def site_id(high, z, core, y, low):
    return {"frame": high * 16 + z * 2 + core, "space": y * 2 + low}


def meet(peers):
    barrier = pltpu.get_barrier_semaphore()
    for peer in peers:
        pl.semaphore_signal(barrier, inc=1, device_id=peer, device_id_type=MESH)
    pl.semaphore_wait(barrier, len(peers))


def frame_peer(distance):
    return {"frame": (lax.axis_index("frame") + distance) % 32, "space": lax.axis_index("space")}


def swap_rows(source, landing, send_sem, recv_sem):
    me = lax.axis_index("frame")
    flying = []
    for distance in range(1, 32):
        peer = frame_peer(distance)
        copy = pltpu.make_async_remote_copy(
            src_ref=source.at[pl.ds(pl.multiple_of(peer["frame"] * SUB, SUB), SUB), :],
            dst_ref=landing.at[pl.ds(pl.multiple_of(me * SUB, SUB), SUB), :],
            send_sem=send_sem.at[distance - 1],
            recv_sem=recv_sem.at[distance - 1],
            device_id=peer,
            device_id_type=MESH,
        )
        copy.start()
        flying.append(copy)
    here = pl.ds(pl.multiple_of(me * SUB, SUB), SUB)
    landing[here, :] = source[here, :]
    return flying


def gather_kernel(
    proj_s, out_s, proj_t, out_t, facts, own_out, rest_out, facts_out,
    own_main, own_rest, main, rest, tail_s, tail_t, landing, send_sem, recv_sem, swap_send, swap_recv,
):
    high, z, core, y, low = sites()
    up = site_id(high, (z + 1) % 8, core, y, low)
    down = site_id(high, (z + 7) % 8, core, y, low)
    across = site_id(1 - high, z, core, y, 1 - low)
    north = site_id(high, z, core, (y + 1) % 4, low)
    south = site_id(high, z, core, (y + 3) % 4, low)
    sibling = site_id(high, z, 1 - core, y, low)
    meet([across, north, south] + [frame_peer(distance) for distance in range(1, 32)])
    swapped = swap_rows(facts, landing, swap_send, swap_recv)

    def slot(half, level):
        return half * 16 + (level % 8) * 2 + core

    mine = slot(high, z)
    group = y
    span = HEADS // GROUPS * HEAD
    width = HEADS * HEAD
    source = lax.broadcasted_iota(jnp.int32, (width, span), 0)
    target = lax.broadcasted_iota(jnp.int32, (width, span), 1)
    chosen = jnp.where(source == target + group * span, 1.0, 0.0).astype(jnp.bfloat16)
    here = pl.ds(pl.multiple_of(mine * TOP, TOP), TOP)
    for part in range(3):
        piece = jnp.dot(
            proj_s[:, part * width : (part + 1) * width], chosen, preferred_element_type=jnp.float32
        )
        own_main[here, part * span : (part + 1) * span] = piece[:TOP].astype(jnp.bfloat16)
        tail_s[0:4, part * span : (part + 1) * span] = piece[TOP:]
    own_main[here, 3 * span :] = jnp.zeros((TOP, own_main.shape[1] - 3 * span), jnp.bfloat16)
    tail_s[0:4, 3 * span :] = jnp.zeros((4, tail_s.shape[1] - 3 * span), jnp.float32)
    first = 0
    for piece in (out_s, proj_t, out_t):
        columns = pl.ds(first, piece.shape[1])
        main[here, columns] = piece[:TOP, :]
        tail_t[0:4, columns] = piece[TOP:, :].astype(jnp.float32)
        first += piece.shape[1]
    tail_t[0:4, first:] = jnp.zeros((4, tail_t.shape[1] - first), jnp.float32)
    below = pl.ds(pl.multiple_of(mine * TILE, TILE), TILE)
    for packed, tail in ((own_rest, tail_s), (rest, tail_t)):
        size = packed.shape[1]
        quarters = [tail[0:4, a * size : (a + 1) * size] for a in range(4)]
        packed[below, :] = jnp.concatenate(quarters, 0).astype(jnp.bfloat16)

    arrays = ((own_main, TOP), (own_rest, TILE), (main, TOP), (rest, TILE))
    started = []

    def copies(kind, which, peer, index, half=None):
        made = []
        for number in (2 * kind, 2 * kind + 1):
            array, rows = arrays[number]
            first, count = which * rows, rows
            if half is not None:
                if rows == TOP:
                    first, count = first + half * TILE, TILE
                elif half == 1:
                    continue
            piece = array.at[pl.ds(pl.multiple_of(first, TILE), count), :]
            made.append(
                pltpu.make_async_remote_copy(
                    src_ref=piece,
                    dst_ref=piece,
                    send_sem=send_sem.at[index, number],
                    recv_sem=recv_sem.at[index, number],
                    device_id=peer,
                    device_id_type=MESH,
                )
            )
        return made

    def send(kind, which, peer, index, half=None):
        for copy in copies(kind, which, peer, index, half):
            copy.start()
            started.append(copy)

    def arrive(kind, which, peer, index, half=None):
        for copy in copies(kind, which, peer, index, half):
            copy.wait_recv()

    HANDED, ACROSS = 16, 32
    handed = ([], [])

    def hand(kind, which):
        send(kind, which, sibling, HANDED + len(handed[kind]))
        handed[kind].append(which)

    def ring(kind, reach):
        for hop in range(1, 5):
            half = (0, 1) if hop == 4 else (None, None)
            lower, upper = slot(high, z + 8 - hop), slot(high, z + hop)
            arrive(kind, lower, up, hop - 1, half[0])
            if hop < 4:
                send(kind, lower, up, hop, 0 if hop == 3 else None)
            arrive(kind, upper, down, 4 + hop - 1, half[1])
            if hop < 4:
                send(kind, upper, down, 4 + hop, 1 if hop == 3 else None)
                hand(kind, lower)
                reach(hop, lower)
            hand(kind, upper)
            reach(hop, upper)

    for kind in (0, 1):
        send(kind, mine, up, 0)
        send(kind, mine, down, 4)
        hand(kind, mine)
        if kind == 0:
            send(kind, mine, across, ACROSS)

    passed = [mine]

    def pass_across(hop, which):
        send(0, which, across, ACROSS + len(passed))
        passed.append(which)

    ring(0, pass_across)
    for index, which in enumerate(passed):
        other = which + 16 - 32 * high
        arrive(0, other, across, ACROSS + index)
        hand(0, other)

    def two_across(hop, which):
        if hop == 2 and len(handed[1]) == 5:
            send(1, slot(high, z + y + 7), across, 8)
        if hop == 4:
            send(1, slot(high, z + y + 3), across, 9)

    ring(1, two_across)
    near, far = slot(1 - high, z + y + 7), slot(1 - high, z + y + 3)
    before, after, opposite = (y + 3) % 4, (y + 1) % 4, (y + 2) % 4
    for which, index in ((near, 0), (far, 1)):
        arrive(1, which, across, 8 + index)
        send(1, which, north, 10 + index)
        send(1, which, south, 12 + index)
        hand(1, which)
    steps = (
        (before, 7, north, 10, 14),
        (after, 7, south, 12, None),
        (after, 3, south, 13, 15),
        (before, 3, north, 11, None),
        (opposite, 7, north, 14, None),
        (opposite, 3, south, 15, None),
    )
    for place, shift, way, index, onward in steps:
        which = slot(1 - high, z + place + shift)
        arrive(1, which, way, index)
        if onward is not None:
            send(1, which, way, onward)
        hand(1, which)
    for kind in (0, 1):
        for index, which in enumerate(handed[kind]):
            arrive(kind, which + 1 - 2 * core, sibling, HANDED + index)
    for copy in started:
        copy.wait_send()
    for copy in swapped:
        copy.wait()
    facts_out[...] = landing[...]

    for top, low_rows, whole in ((own_main, own_rest, own_out), (main, rest, rest_out)):
        size = low_rows.shape[1]
        for quarter in range(4):
            lo, hi = quarter * size, min((quarter + 1) * size, whole.shape[1])
            order = restore_order(quarter)

            @pl.loop(0, 8)
            def _(quad):
                pieces = jnp.concatenate(
                    [
                        top[pl.ds(pl.multiple_of(quad * 4 * TOP, 4 * TOP), 4 * TOP), lo:hi],
                        low_rows[pl.ds(pl.multiple_of(quad * 4 * TILE, 4 * TILE), 4 * TILE), : hi - lo],
                    ],
                    0,
                )
                rows = jnp.dot(order, pieces, preferred_element_type=jnp.float32)
                whole[pl.ds(pl.multiple_of(quad * 144, 16), 144), lo:hi] = rows.astype(jnp.bfloat16)


def restore_order(quarter):
    row = lax.broadcasted_iota(jnp.int32, (144, 4 * TOP + 4 * TILE), 0)
    column = lax.broadcasted_iota(jnp.int32, (144, 4 * TOP + 4 * TILE), 1)
    device, inner = row // 36, row % 36
    source = jnp.where(
        inner < TOP, device * TOP + inner, 4 * TOP + device * TILE + quarter * 4 + inner - TOP
    )
    return jnp.where(source == column, 1.0, 0.0).astype(jnp.bfloat16)


def gather_weights(spatial_proj, spatial_out, temporal_proj, temporal_out, facts):
    width = HEADS * HEAD
    own, other = 7 * LANES, 5 * width
    packed = (2 * LANES, 12 * LANES)
    return pl.pallas_call(
        gather_kernel,
        out_shape=[
            jax.ShapeDtypeStruct((width, own), jnp.bfloat16),
            jax.ShapeDtypeStruct((width, other), jnp.bfloat16),
            jax.ShapeDtypeStruct(facts.shape, jnp.float32),
        ],
        in_specs=[pl.BlockSpec(memory_space=pltpu.VMEM)] * 5,
        out_specs=[pl.BlockSpec(memory_space=pltpu.VMEM)] * 3,
        scratch_shapes=[
            pltpu.VMEM((32 * TOP, own), jnp.bfloat16),
            pltpu.VMEM((32 * TILE, packed[0]), jnp.bfloat16),
            pltpu.VMEM((32 * TOP, other), jnp.bfloat16),
            pltpu.VMEM((32 * TILE, packed[1]), jnp.bfloat16),
            pltpu.VMEM((SUB, 4 * packed[0]), jnp.float32),
            pltpu.VMEM((SUB, 4 * packed[1]), jnp.float32),
            pltpu.VMEM(facts.shape, jnp.float32),
            pltpu.SemaphoreType.DMA((40, 4)),
            pltpu.SemaphoreType.DMA((40, 4)),
            pltpu.SemaphoreType.DMA((31,)),
            pltpu.SemaphoreType.DMA((31,)),
        ],
        compiler_params=pltpu.CompilerParams(
            collective_id=0, has_side_effects=True, vmem_limit_bytes=VMEM_BYTES
        ),
        name="gather",
    )(spatial_proj, spatial_out, temporal_proj, temporal_out, facts)


def head_scale(values):
    return lax.rsqrt(jnp.mean(values * values, -1, keepdims=True) + epsilon)


def one_column(rows):
    lane = lax.broadcasted_iota(jnp.int32, (rows, LANES - HEAD), 1)
    return jnp.where(lane == 0, 1.0, 0.0).astype(jnp.bfloat16)


def contract_last(left, right):
    return lax.dot_general(
        left, right, (((1,), (1,)), ((), ())), preferred_element_type=jnp.float32
    )


def spatial_kernel(
    latents, features, time_proj, embed, weights, out,
    tokens, mixed, parts, stage, landing, triple, qs, ks, vs,
    share_send, share_recv, part_send, part_recv, row_send, row_recv,
):
    high, z, core, y, low = sites()
    place = y * 2 + low
    width, local_heads = HEADS * HEAD, HEADS // GROUPS
    span = local_heads * HEAD

    def plane_peer(dy, a, b, c):
        return site_id((high + b) % 2, z, (core + c) % 2, (y + dy) % 4, (low + a) % 2)

    offsets = [(dy, a, b, c) for dy in range(4) for a in range(2) for b in range(2) for c in range(2)]
    above = [site_id(high, (z + d) % 8, core, y, low) for d in range(1, 8)]
    meet([plane_peer(*offset) for offset in offsets[1:]] + above)

    shares = []
    mine = pl.ds(pl.multiple_of(place * LANES, LANES), LANES)
    for d in range(1, 8):
        other = (place + d) % 8
        copy = pltpu.make_async_remote_copy(
            src_ref=latents.at[other % 2],
            dst_ref=tokens.at[mine, :],
            send_sem=share_send.at[d - 1],
            recv_sem=share_recv.at[d - 1],
            device_id={"frame": lax.axis_index("frame"), "space": other},
            device_id_type=MESH,
        )
        copy.start()
        shares.append(copy)
    tokens[mine, :] = latents[low]
    mods = jnp.dot(features[...], time_proj[:, : 2 * width], preferred_element_type=jnp.float32)
    shift, scale = mods[:1, :width], 1.0 + mods[:1, width:]
    mixed[:, span:] = jnp.zeros((mixed.shape[0], mixed.shape[1] - span), jnp.bfloat16)
    for copy in shares:
        copy.wait()

    rows = tokens.shape[0]
    for first in range(0, rows, BLOCK):
        here = pl.ds(first, BLOCK)
        hidden = jnp.dot(tokens[here, :PATCH], embed[...], preferred_element_type=jnp.float32)
        normed = layer_norm(hidden) * scale + shift
        triple[...] = jnp.dot(
            normed.astype(jnp.bfloat16), weights[...], preferred_element_type=jnp.float32
        )
        for head in range(local_heads):
            query = triple[:, head * HEAD : (head + 1) * HEAD]
            key = triple[:, (local_heads + head) * HEAD : (local_heads + head + 1) * HEAD]
            value = triple[:, (2 * local_heads + head) * HEAD : (2 * local_heads + head + 1) * HEAD]
            qs[head, here, :] = (query * (head_scale(query) * SHARPEN)).astype(jnp.bfloat16)
            ks[head, here, :] = (key * head_scale(key)).astype(jnp.bfloat16)
            vs[head, here, :HEAD] = value.astype(jnp.bfloat16)
            vs[head, here, HEAD:] = one_column(BLOCK)

    sent = []
    own_part = pl.ds(pl.multiple_of((high * 4 + core * 2 + low) * 32, 32), 32)
    for dy in range(4):
        first = (y + dy) % 4 * BLOCK
        here = pl.ds(pl.multiple_of(first, BLOCK), BLOCK)
        for head in range(local_heads):
            raised = jnp.exp2(contract_last(qs[head, here, :], ks[head])).astype(jnp.bfloat16)
            mix = jnp.dot(raised, vs[head], preferred_element_type=jnp.float32)
            mix = mix[:, :HEAD] / mix[:, HEAD : HEAD + 1]
            mixed[here, head * HEAD : (head + 1) * HEAD] = mix.astype(jnp.bfloat16)
        for index, (step, a, b, c) in enumerate(offsets):
            if step != dy:
                continue
            target = (low + a) % 2 * 4 + (high + b) % 2 * 2 + (core + c) % 2
            piece = pl.ds(pl.multiple_of(first + target * 32, 32), 32)
            if index == 0:
                parts[y, own_part, :] = mixed[piece, :]
                continue
            copy = pltpu.make_async_remote_copy(
                src_ref=mixed.at[piece, :],
                dst_ref=parts.at[y, own_part, :],
                send_sem=part_send.at[index - 1],
                recv_sem=part_recv.at[index - 1],
                device_id=plane_peer(step, a, b, c),
                device_id_type=MESH,
            )
            copy.start()
            sent.append(copy)
    for copy in sent:
        copy.wait()

    target = lax.broadcasted_iota(jnp.int32, (2 * LANES, 2 * LANES), 0)
    source = lax.broadcasted_iota(jnp.int32, (2 * LANES, 2 * LANES), 1)
    moved = target % 32 // 8 * 64 + target % 2 * 32 + target // 32 * 4 + target % 8 // 2
    order = jnp.where(moved == source, 1.0, 0.0).astype(jnp.bfloat16)
    for group in range(GROUPS):
        piece = jnp.dot(order, parts[group], preferred_element_type=jnp.float32)
        stage[:, group * span : (group + 1) * span] = piece[:, :span].astype(jnp.bfloat16)
    flying = []
    for d in range(1, 8):
        for half in range(2):
            origin = pl.ds(pl.multiple_of((z + d) % 8 * 32 + half * TILE, TILE), TILE)
            goal = pl.ds(pl.multiple_of(half * LANES + z * TILE, TILE), TILE)
            copy = pltpu.make_async_remote_copy(
                src_ref=stage.at[origin, :],
                dst_ref=landing.at[goal, :],
                send_sem=row_send.at[d - 1, half],
                recv_sem=row_recv.at[d - 1, half],
                device_id=above[d - 1],
                device_id_type=MESH,
            )
            copy.start()
            flying.append(copy)
    for half in range(2):
        origin = pl.ds(pl.multiple_of(z * 32 + half * TILE, TILE), TILE)
        goal = pl.ds(pl.multiple_of(half * LANES + z * TILE, TILE), TILE)
        landing[goal, :] = stage[origin, :]
    for copy in flying:
        copy.wait()
    out[...] = landing[...]


def spatial_block(latents, features, time_proj, embed_in, weights):
    width, local_heads, rows = HEADS * HEAD, HEADS // GROUPS, 8 * LANES
    vmem = pl.BlockSpec(memory_space=pltpu.VMEM)
    return pl.pallas_call(
        spatial_kernel,
        out_shape=jax.ShapeDtypeStruct((2 * LANES, width), jnp.bfloat16),
        in_specs=[vmem] * 5,
        out_specs=vmem,
        scratch_shapes=[
            pltpu.VMEM((rows, LANES), jnp.bfloat16),
            pltpu.VMEM((rows, 3 * LANES), jnp.bfloat16),
            pltpu.VMEM((GROUPS, 2 * LANES, 3 * LANES), jnp.bfloat16),
            pltpu.VMEM((2 * LANES, width), jnp.bfloat16),
            pltpu.VMEM((2 * LANES, width), jnp.bfloat16),
            pltpu.VMEM((BLOCK, weights.shape[1]), jnp.float32),
            pltpu.VMEM((local_heads, rows, HEAD), jnp.bfloat16),
            pltpu.VMEM((local_heads, rows, HEAD), jnp.bfloat16),
            pltpu.VMEM((local_heads, rows, LANES), jnp.bfloat16),
            pltpu.SemaphoreType.DMA((7,)),
            pltpu.SemaphoreType.DMA((7,)),
            pltpu.SemaphoreType.DMA((31,)),
            pltpu.SemaphoreType.DMA((31,)),
            pltpu.SemaphoreType.DMA((7, 2)),
            pltpu.SemaphoreType.DMA((7, 2)),
        ],
        compiler_params=pltpu.CompilerParams(
            collective_id=1, has_side_effects=True, vmem_limit_bytes=VMEM_BYTES
        ),
        name="spatial",
    )(latents, features, time_proj, embed_in, weights)


def temporal_kernel(
    last, offset, mixed, facts, state, fresh, time_proj, embed_in, shared, embed_out, *rest,
):
    if last:
        queue, velocities, outgoing, landing, triple, mix, send_sem, recv_sem = rest
    else:
        latents, outgoing, landing, triple, mix, send_sem, recv_sem = rest
    meet([frame_peer(distance) for distance in range(1, 32)])
    rows, width = mixed.shape[0], HEADS * HEAD
    features = facts[:, LANES:].astype(jnp.bfloat16)

    def mod(part):
        columns = time_proj[:, part * width : (part + 1) * width]
        return jnp.dot(features, columns, preferred_element_type=jnp.float32)

    hidden_in = jnp.dot(
        state[:, :PATCH].astype(jnp.bfloat16), embed_in[...], preferred_element_type=jnp.float32
    )
    back = jnp.dot(mixed[...], shared[:, :width], preferred_element_type=jnp.float32)
    hidden = hidden_in + mod(2) * back
    normed = layer_norm(hidden) * (1.0 + mod(4)) + mod(3)
    triple[...] = jnp.dot(
        normed.astype(jnp.bfloat16), shared[:, width : 4 * width], preferred_element_type=jnp.float32
    )

    def place(index):
        frame = index // SUB * 2 + index % 2
        return (frame + WIN - offset[0]) // WIN, index % SUB // 2

    window_row, token_row = place(lax.broadcasted_iota(jnp.int32, (rows, rows), 0))
    window_col, token_col = place(lax.broadcasted_iota(jnp.int32, (rows, rows), 1))
    same = (window_row == window_col) & (token_row == token_col)
    ones = one_column(rows)
    for head in range(HEADS):
        query = triple[:, head * HEAD : (head + 1) * HEAD]
        key = triple[:, width + head * HEAD : width + (head + 1) * HEAD]
        value = triple[:, 2 * width + head * HEAD : 2 * width + (head + 1) * HEAD]
        query = (query * (head_scale(query) * SHARPEN)).astype(jnp.bfloat16)
        key = (key * head_scale(key)).astype(jnp.bfloat16)
        value = jnp.concatenate([value.astype(jnp.bfloat16), ones], -1)
        raised = jnp.where(same, jnp.exp2(contract_last(query, key)), 0.0).astype(jnp.bfloat16)
        part = jnp.dot(raised, value, preferred_element_type=jnp.float32)
        part = part[:, :HEAD] / part[:, HEAD : HEAD + 1]
        mix[:, head * HEAD : (head + 1) * HEAD] = part.astype(jnp.bfloat16)
    forth = jnp.dot(mix[...], shared[:, 4 * width :], preferred_element_type=jnp.float32)
    hidden = hidden + mod(5) * forth
    velocity = jnp.dot(
        layer_norm(hidden).astype(jnp.bfloat16), embed_out[...], preferred_element_type=jnp.float32
    )
    stepped = state[:, :PATCH] + facts[:, PATCH : PATCH + 1] * velocity
    outgoing[:, 3 * PATCH :] = jnp.zeros((rows, LANES - 3 * PATCH), jnp.float32)
    if last:
        outgoing[:, :PATCH] = stepped
        outgoing[:, PATCH : 2 * PATCH] = state[:, PATCH : 2 * PATCH]
        outgoing[:, 2 * PATCH : 3 * PATCH] = velocity
    else:
        outgoing[:, PATCH : 2 * PATCH] = velocity
        outgoing[:, 2 * PATCH : 3 * PATCH] = jnp.zeros((rows, PATCH), jnp.float32)
        outgoing[:, :PATCH] = stepped
        wide = outgoing[...]
        index = lax.broadcasted_iota(jnp.int32, (rows, LANES), 0)
        first = index % 2 == 0
        ahead = jnp.where(first, pltpu.roll(wide, rows - 1, 0), pltpu.roll(wide, rows - 7, 0))
        tail = jnp.concatenate([fresh[...]] * (rows // SUB), 0)
        ahead = jnp.where(first | (index < rows - SUB), ahead, tail)
        outgoing[:, :PATCH] = ahead[:, :PATCH]
    for copy in swap_rows(outgoing, landing, send_sem, recv_sem):
        copy.wait()
    if last:
        for j in range(2):
            piece = landing[pl.ds(j, LANES, stride=2), :]
            queue[j] = piece[:, :PATCH]
            velocities[0, j] = piece[:, PATCH : 2 * PATCH]
            velocities[1, j] = piece[:, 2 * PATCH : 3 * PATCH]
    else:
        target = lax.broadcasted_iota(jnp.int32, (LANES, 2 * LANES), 0)
        source = lax.broadcasted_iota(jnp.int32, (LANES, 2 * LANES), 1)
        moved = target // 64 * 16 + target % 32 // 4 * 2 + target // 32 % 2
        moved = moved * SUB + target % 4 * 2
        lane = lax.broadcasted_iota(jnp.int32, (rows, LANES), 1)
        clean = jnp.where(lane < PATCH, landing[...], 0.0).astype(jnp.bfloat16)
        for j in range(2):
            order = jnp.where(moved + j == source, 1.0, 0.0).astype(jnp.bfloat16)
            latents[j] = jnp.dot(order, clean, preferred_element_type=jnp.float32).astype(
                jnp.bfloat16
            )


def temporal_block(last, offset, mixed, facts, state, fresh, time_proj, embed_in, shared, embed_out):
    width, rows = HEADS * HEAD, mixed.shape[0]
    vmem = pl.BlockSpec(memory_space=pltpu.VMEM)
    local = (2, LANES, PATCH)
    if last:
        shapes = [
            jax.ShapeDtypeStruct(local, jnp.float32),
            jax.ShapeDtypeStruct((STEPS, *local), jnp.float32),
        ]
        scratch = [pltpu.VMEM((rows, LANES), jnp.float32)]
    else:
        shapes = [
            jax.ShapeDtypeStruct((2, LANES, LANES), jnp.bfloat16),
            jax.ShapeDtypeStruct((rows, LANES), jnp.float32),
        ]
        scratch = []
    return pl.pallas_call(
        functools.partial(temporal_kernel, last),
        out_shape=shapes,
        in_specs=[pl.BlockSpec(memory_space=pltpu.SMEM)]
        + [vmem] * 8,
        out_specs=[vmem] * 2,
        scratch_shapes=scratch
        + [
            pltpu.VMEM((rows, LANES), jnp.float32),
            pltpu.VMEM((rows, 3 * width), jnp.float32),
            pltpu.VMEM((rows, width), jnp.bfloat16),
            pltpu.SemaphoreType.DMA((31,)),
            pltpu.SemaphoreType.DMA((31,)),
        ],
        compiler_params=pltpu.CompilerParams(
            collective_id=3 if last else 2, has_side_effects=True, vmem_limit_bytes=VMEM_BYTES
        ),
        name="temporal",
    )(offset[None], mixed, facts, state, fresh, time_proj, embed_in, shared, embed_out)


def row_facts(latents, step_size, features):
    count, tokens, size = latents.shape
    rows = latents.reshape(count, 32, tokens // 32, size)
    rows = jnp.transpose(rows, (1, 2, 0, 3)).reshape(2 * tokens, size)
    steps = jnp.broadcast_to(step_size[None], (tokens, count)).reshape(2 * tokens, 1)
    wide = jnp.broadcast_to(features.astype(jnp.float32)[None], (tokens, count, 2 * LANES))
    gap = jnp.zeros((2 * tokens, LANES - size - 1), jnp.float32)
    return jnp.concatenate([rows, steps, gap, wide.reshape(2 * tokens, 2 * LANES)], -1)


def plane_rows(latents):
    rows = latents.astype(jnp.bfloat16).reshape(2, 2, 8, 2, 4, PATCH)
    rows = jnp.swapaxes(rows, 2, 3).reshape(2, LANES, PATCH)
    return jnp.pad(rows, ((0, 0), (0, 0), (0, LANES - PATCH)))


def local(
    latents,
    fresh_noise,
    levels,
    timesteps,
    window_offsets,
    time_proj,
    embed_in,
    spatial_proj,
    spatial_out,
    temporal_proj,
    temporal_out,
    embed_out,
):
    which, row = lax.axis_index("space") % 2, lax.axis_index("frame")
    time_value = lookup_table(levels, timesteps)
    earlier = lookup_table(levels - 1, timesteps)
    features = time_features(time_value, time_proj.shape[0] // 2)
    facts = row_facts(latents, (earlier - time_value) / 1000.0, features)
    spatial_own, shared, facts = gather_weights(
        spatial_proj, spatial_out, temporal_proj, temporal_out, facts
    )
    own = jnp.broadcast_to(lax.dynamic_index_in_dim(features, which, 0), (TILE, 2 * LANES))
    fresh = lax.dynamic_slice_in_dim(fresh_noise[0], row * 4, 4)
    fresh = jnp.pad(jnp.repeat(fresh, 2, axis=0), ((0, 0), (0, LANES - PATCH)))
    tokens, state = plane_rows(latents), facts[:, :LANES]
    for step_index in range(STEPS):
        mixed = spatial_block(tokens, own, time_proj, embed_in, spatial_own)
        tokens, state = temporal_block(
            step_index == STEPS - 1,
            window_offsets[step_index],
            mixed,
            facts,
            state,
            fresh,
            time_proj,
            embed_in,
            shared,
            embed_out,
        )
    return tokens, state


def solution(mesh):
    return jax.shard_map(
        local,
        mesh=mesh,
        in_specs=(
            P("frame", "space", None),
            P(None, "space", None),
            P("frame"),
            P(),
            P(),
            P(),
            P(),
            P("frame", None),
            P("frame", None),
            P("frame", None),
            P("frame", None),
            P(),
        ),
        out_specs=(P("frame", "space", None), P(None, "frame", "space", None)),
        check_vma=False,
    )
```

```python
import functools
import math

import jax
import jax.numpy as jnp
from jax import lax
from jax.experimental import pallas as pl
from jax.experimental.pallas import tpu as pltpu
from jax.sharding import PartitionSpec as P

HEADS = 16
HEAD = 72
WIN = 16
STEPS = 2
PATCH = 16
GROUPS = 4
LANES = 128
SUB = 8
TILE = 16
TOP = 32
MESH = pl.DeviceIdType.MESH
CHUNKS = ((0, 8), (8, 33), (33, 59))
HANDED, ACROSS = 16, 32
BLOCK = 256
SHARPEN = HEAD ** (-0.5) * math.log2(math.e)
VMEM_BYTES = 61 * 2**20


epsilon = 1e-06


def layer_norm(values):
    center = values - jnp.mean(values, -1, keepdims=True)
    spread = jnp.mean(center * center, -1, keepdims=True)
    return center * lax.rsqrt(spread + epsilon)


def lookup_table(indices, table):
    hits = indices[:, None] == jnp.arange(table.shape[0], dtype=jnp.int32)[None, :]
    return jnp.sum(jnp.where(hits, table[None, :], 0), axis=1).astype(jnp.float32)


def time_features(time_value, half):
    freqs = jnp.exp(-math.log(10000.0) * jnp.arange(half, dtype=jnp.float32) / half)
    angles = time_value[:, None] * freqs[None, :]
    return jnp.concatenate([jnp.cos(angles), jnp.sin(angles)], -1).astype(jnp.bfloat16)


def head_scale(values):
    return lax.rsqrt(jnp.mean(values * values, -1, keepdims=True) + epsilon)


def one_column(rows):
    lane = lax.broadcasted_iota(jnp.int32, (rows, LANES - HEAD), 1)
    return jnp.where(lane == 0, 1.0, 0.0).astype(jnp.bfloat16)


def contract_last(left, right):
    return lax.dot_general(
        left, right, (((1,), (1,)), ((), ())), preferred_element_type=jnp.float32
    )


def sites():
    frame, space = lax.axis_index("frame"), lax.axis_index("space")
    return frame // 16, frame // 2 % 8, frame % 2, space // 2, space % 2


def site_id(high, z, core, y, low):
    return {"frame": high * 16 + z * 2 + core, "space": y * 2 + low}


def meet(peers):
    barrier = pltpu.get_barrier_semaphore()
    for peer in peers:
        pl.semaphore_signal(barrier, inc=1, device_id=peer, device_id_type=MESH)
    pl.semaphore_wait(barrier, len(peers))


def swap_rows(source, landing, send_sem, recv_sem):
    me, space = lax.axis_index("frame"), lax.axis_index("space")
    here = pl.ds(pl.multiple_of(me * SUB, SUB), SUB)
    flying = []
    for distance in range(1, 32):
        peer = (me + distance) % 32
        flying.append(
            remote(
                source.at[pl.ds(pl.multiple_of(peer * SUB, SUB), SUB), :],
                landing.at[here, :],
                send_sem.at[distance - 1],
                recv_sem.at[distance - 1],
                {"frame": peer, "space": space},
            )
        )
    for copy in flying:
        copy.start()
    landing[here, :] = source[here, :]
    return flying


def remote(source, target, send_sem, recv_sem, peer):
    return pltpu.make_async_remote_copy(
        src_ref=source,
        dst_ref=target,
        send_sem=send_sem,
        recv_sem=recv_sem,
        device_id=peer,
        device_id_type=MESH,
    )


def restore_order(quarter):
    row = lax.broadcasted_iota(jnp.int32, (144, 4 * TOP + 4 * TILE), 0)
    column = lax.broadcasted_iota(jnp.int32, (144, 4 * TOP + 4 * TILE), 1)
    device, inner = row // 36, row % 36
    source = jnp.where(
        inner < TOP, device * TOP + inner, 4 * TOP + device * TILE + quarter * 4 + inner - TOP
    )
    return jnp.where(source == column, 1.0, 0.0).astype(jnp.bfloat16)


class Gather:
    def __init__(self, blocks, send_sem, recv_sem):
        self.blocks, self.send_sem, self.recv_sem = blocks, send_sem, recv_sem
        high, z, core, y, low = sites()
        self.place = (high, z, core, y, low)
        self.up = site_id(high, (z + 1) % 8, core, y, low)
        self.down = site_id(high, (z + 7) % 8, core, y, low)
        self.across = site_id(1 - high, z, core, y, 1 - low)
        self.north = site_id(high, z, core, (y + 1) % 4, low)
        self.south = site_id(high, z, core, (y + 3) % 4, low)
        self.sibling = site_id(high, z, 1 - core, y, low)
        self.mine = self.slot(high, z)
        self.handed = ([], [], [])
        self.passed = []
        self.started = []

    def slot(self, half, level):
        return half * 16 + level % 8 * 2 + self.place[2]

    def copy(self, kind, which, peer, index, half=None):
        first, last = CHUNKS[kind]
        if half is not None:
            middle = (first + last) // 2
            first, last = (first, middle) if half == 0 else (middle, last)
        piece = self.blocks.at[which, first:last]
        return remote(
            piece, piece, self.send_sem.at[index, kind], self.recv_sem.at[index, kind], peer
        )

    def send(self, kind, which, peer, index, half=None):
        copy = self.copy(kind, which, peer, index, half)
        copy.start()
        self.started.append(copy)

    def arrive(self, kind, which, peer, index, half=None):
        self.copy(kind, which, peer, index, half).wait_recv()

    def hand(self, kind, which):
        self.send(kind, which, self.sibling, HANDED + len(self.handed[kind]))
        self.handed[kind].append(which)

    def begin(self, kind):
        self.send(kind, self.mine, self.up, 0)
        self.send(kind, self.mine, self.down, 4)
        if kind == 0:
            self.pass_across(self.mine)
        self.hand(kind, self.mine)

    def pass_across(self, which):
        self.send(0, which, self.across, ACROSS + len(self.passed))
        self.passed.append(which)

    def hop(self, kind, hop):
        high, z, core, y, low = self.place
        half = (0, 1) if hop == 4 else (None, None)
        lower, upper = self.slot(high, z + 8 - hop), self.slot(high, z + hop)
        self.arrive(kind, lower, self.up, hop - 1, half[0])
        if hop < 4:
            self.send(kind, lower, self.up, hop, 0 if hop == 3 else None)
        self.arrive(kind, upper, self.down, 4 + hop - 1, half[1])
        if hop < 4:
            self.send(kind, upper, self.down, 4 + hop, 1 if hop == 3 else None)
        if kind == 0:
            for which in (lower, upper)[hop // 4 :]:
                self.pass_across(which)
        elif hop == 2:
            self.send(kind, self.slot(high, z + y + 7), self.across, 8)
        elif hop == 4:
            self.send(kind, self.slot(high, z + y + 3), self.across, 9)
        for which in (lower, upper)[hop // 4 :]:
            self.hand(kind, which)

    def finish_own(self):
        for index, which in enumerate(self.passed):
            other = which + 16 - 32 * self.place[0]
            self.arrive(0, other, self.across, ACROSS + index)
            self.hand(0, other)

    def cross(self, kind, far):
        high, z, core, y, low = self.place
        which = self.slot(1 - high, z + y + (3 if far else 7))
        self.arrive(kind, which, self.across, 8 + far)
        self.send(kind, which, self.north, 10 + far)
        self.send(kind, which, self.south, 12 + far)
        self.hand(kind, which)

    def round_y(self, kind, step):
        high, z, core, y, low = self.place
        turn, shift, north, index, onward = (
            (3, 7, True, 10, 14),
            (1, 7, False, 12, None),
            (1, 3, False, 13, 15),
            (3, 3, True, 11, None),
            (2, 7, True, 14, None),
            (2, 3, False, 15, None),
        )[step]
        way = self.north if north else self.south
        which = self.slot(1 - high, z + (y + turn) % 4 + shift)
        self.arrive(kind, which, way, index)
        if onward is not None:
            self.send(kind, which, way, onward)
        self.hand(kind, which)

    def collect(self, kind):
        for index, which in enumerate(self.handed[kind]):
            self.arrive(kind, which + 1 - 2 * self.place[2], self.sibling, HANDED + index)

    def events(self):
        kinds = (1, 2)
        plan = [functools.partial(self.hop, kind, hop) for hop in (1, 2, 3) for kind in kinds]
        plan += [functools.partial(self.cross, kind, 0) for kind in kinds]
        plan += [functools.partial(self.hop, kind, 4) for kind in kinds]
        plan += [functools.partial(self.round_y, kind, step) for step in (0, 1) for kind in kinds]
        plan += [functools.partial(self.cross, kind, 1) for kind in kinds]
        plan += [functools.partial(self.round_y, kind, step) for step in (4, 2, 3, 5) for kind in kinds]
        return plan


def pack_rows(blocks, mine, first, tail, pieces):
    tile = 0
    for count, top, low in pieces:
        for number in range(count):
            blocks[mine, first + tile] = top(number)
            tail[0:4, tile * LANES : (tile + 1) * LANES] = low(number)
            tile += 1
    total = tail.shape[1] // LANES
    if total > tile:
        tail[0:4, tile * LANES :] = jnp.zeros((4, (total - tile) * LANES), jnp.float32)
    quarter = total // 4
    rest = first + tile
    for number in range(quarter):
        rows = [
            tail[0:4, (a * quarter + number) * LANES : (a * quarter + number + 1) * LANES]
            for a in range(4)
        ]
        packed = jnp.concatenate(rows, 0).astype(jnp.bfloat16)
        blocks[mine, rest + number // 2, number % 2 * TILE : (number % 2 + 1) * TILE, :] = packed


def restore_rows(blocks, whole, first, tiles, quarter):
    rest = first + tiles
    for a in range(4):
        order = restore_order(a)
        start, stop = a * quarter, min((a + 1) * quarter, tiles)

        @pl.loop(0, 8)
        def _(quad):
            four = pl.ds(quad * 4, 4)
            rows = pl.ds(pl.multiple_of(quad * 144, 16), 144)
            for begin in range(start, stop, 4):
                end = min(begin + 4, stop)
                columns = []
                for tile in range(begin, end):
                    number = tile - start
                    low = blocks[
                        four, rest + number // 2, number % 2 * TILE : (number % 2 + 1) * TILE, :
                    ]
                    top = blocks[four, first + tile]
                    columns.append(
                        jnp.concatenate(
                            [top.reshape(4 * TOP, LANES), low.reshape(4 * TILE, LANES)], 0
                        )
                    )
                joined = jnp.concatenate(columns, 1)
                result = jnp.dot(order, joined, preferred_element_type=jnp.float32)
                whole[rows, begin * LANES : end * LANES] = result.astype(jnp.bfloat16)


def network_kernel(
    offsets, latents, features, facts, fresh, time_proj, embed_in, embed_out,
    proj_s, out_s, proj_t, out_t, queue, velocities,
    blocks, tail, own, shared, info, mods, tokens, mixed, parts, stage, landing,
    state, outgoing, back, again, triple, qs, ks, vs, mix,
    gather_send, gather_recv, fact_send, fact_recv, share_send, share_recv,
    part_send, part_recv, row_send, row_recv, swap_send, swap_recv,
):
    high, z, core, y, low = sites()
    place, row = y * 2 + low, lax.axis_index("frame")
    width, local_heads = HEADS * HEAD, HEADS // GROUPS
    span = local_heads * HEAD

    def plane_peer(dy, a, b, c):
        return site_id((high + b) % 2, z, (core + c) % 2, (y + dy) % 4, (low + a) % 2)

    offs = [(dy, a, b, c) for dy in range(4) for a in range(2) for b in range(2) for c in range(2)]
    above = [site_id(high, (z + d) % 8, core, y, low) for d in range(1, 8)]
    frames = [(h, d, c) for h in range(2) for d in range(1, 8) for c in range(2)]
    meet(
        [plane_peer(*offset) for offset in offs[1:]]
        + [site_id((high + h) % 2, (z + d) % 8, (core + c) % 2, y, low) for h, d, c in frames]
    )

    gather = Gather(blocks, gather_send, gather_recv)
    source = lax.broadcasted_iota(jnp.int32, (width, span), 0)
    target = lax.broadcasted_iota(jnp.int32, (width, span), 1)
    chosen = jnp.where(source == target + y * span, 1.0, 0.0).astype(jnp.bfloat16)
    own_rows = triple
    for part in range(3):
        own_rows[0:36, part * span : (part + 1) * span] = jnp.dot(
            proj_s[:, part * width : (part + 1) * width], chosen, preferred_element_type=jnp.float32
        )
    own_rows[0:36, 3 * span : 7 * LANES] = jnp.zeros((36, 7 * LANES - 3 * span), jnp.float32)

    def wide_piece(number):
        return own_rows[0:TOP, number * LANES : (number + 1) * LANES].astype(jnp.bfloat16)

    def wide_rest(number):
        return own_rows[TOP:36, number * LANES : (number + 1) * LANES]

    pack_rows(blocks, gather.mine, 0, tail.at[:, : 8 * LANES], [(7, wide_piece, wide_rest)])
    gather.begin(0)

    def pieces(ref):
        return (
            ref.shape[1] // LANES,
            lambda number: ref[:TOP, number * LANES : (number + 1) * LANES],
            lambda number: ref[TOP:, number * LANES : (number + 1) * LANES].astype(jnp.float32),
        )

    pack_rows(blocks, gather.mine, 8, tail, [pieces(out_s), pieces(proj_t), pieces(out_t)])
    gather.begin(1)
    gather.begin(2)

    mine = pl.ds(pl.multiple_of(place * LANES, LANES), LANES)

    def share(step, source):
        flying = []
        for d in range(1, 8):
            other = (place + d) % 8
            copy = remote(
                source.at[other % 2],
                tokens.at[step, mine, :],
                share_send.at[step, d - 1],
                share_recv.at[step, d - 1],
                {"frame": row, "space": other},
            )
            copy.start()
            flying.append(copy)
        tokens[step, mine, :] = source[low]
        return flying

    shares = share(0, latents)
    fact_copies = swap_rows(facts, info, fact_send, fact_recv)
    plan = gather.events()

    def advance(count):
        for _ in range(min(count, len(plan))):
            plan.pop(0)()

    gather.hop(0, 1)
    gather.hop(0, 2)
    advance(1)
    gather.hop(0, 3)
    advance(1)
    gather.hop(0, 4)
    gather.finish_own()
    gather.collect(0)
    restore_rows(blocks, own, 0, 7, 2)
    first_mods = jnp.dot(features[...], time_proj[:, : 2 * width], preferred_element_type=jnp.float32)
    shift, scale = first_mods[:1, :width], 1.0 + first_mods[:1, width:]
    mixed[:, :, span:] = jnp.zeros((STEPS, 8 * LANES, 3 * LANES - span), jnp.bfloat16)

    def spatial(step, shares, between):
        for copy in shares:
            copy.wait()
        for first in range(0, 8 * LANES, BLOCK):
            here = pl.ds(first, BLOCK)
            hidden = jnp.dot(
                tokens[step, here, :PATCH], embed_in[...], preferred_element_type=jnp.float32
            )
            normed = layer_norm(hidden) * scale + shift
            triple[:, : 7 * LANES] = jnp.dot(
                normed.astype(jnp.bfloat16), own[...], preferred_element_type=jnp.float32
            )
            for head in range(local_heads):
                query = triple[:, head * HEAD : (head + 1) * HEAD]
                key = triple[:, span + head * HEAD : span + (head + 1) * HEAD]
                value = triple[:, 2 * span + head * HEAD : 2 * span + (head + 1) * HEAD]
                qs[head, here, :] = (query * (head_scale(query) * SHARPEN)).astype(jnp.bfloat16)
                ks[head, here, :] = (key * head_scale(key)).astype(jnp.bfloat16)
                vs[head, here, :HEAD] = value.astype(jnp.bfloat16)
                vs[head, here, HEAD:] = one_column(BLOCK)
            between()
        sent = []
        own_part = pl.ds(pl.multiple_of((high * 4 + core * 2 + low) * 32, 32), 32)
        for dy in range(4):
            first = (y + dy) % 4 * BLOCK
            here = pl.ds(pl.multiple_of(first, BLOCK), BLOCK)
            for head in range(local_heads):
                raised = jnp.exp2(contract_last(qs[head, here, :], ks[head])).astype(jnp.bfloat16)
                part = jnp.dot(raised, vs[head], preferred_element_type=jnp.float32)
                part = part[:, :HEAD] / part[:, HEAD : HEAD + 1]
                mixed[step, here, head * HEAD : (head + 1) * HEAD] = part.astype(jnp.bfloat16)
            for index, (way, a, b, c) in enumerate(offs):
                if way != dy:
                    continue
                target = (low + a) % 2 * 4 + (high + b) % 2 * 2 + (core + c) % 2
                piece = pl.ds(pl.multiple_of(first + target * 32, 32), 32)
                if index == 0:
                    parts[step, y, own_part, :] = mixed[step, piece, :]
                    continue
                copy = remote(
                    mixed.at[step, piece, :],
                    parts.at[step, y, own_part, :],
                    part_send.at[step, index - 1],
                    part_recv.at[step, index - 1],
                    plane_peer(way, a, b, c),
                )
                copy.start()
                sent.append(copy)
            between()
        for copy in sent:
            copy.wait()
        target = lax.broadcasted_iota(jnp.int32, (2 * LANES, 2 * LANES), 0)
        source = lax.broadcasted_iota(jnp.int32, (2 * LANES, 2 * LANES), 1)
        moved = target % 32 // 8 * 64 + target % 2 * 32 + target // 32 * 4 + target % 8 // 2
        order = jnp.where(moved == source, 1.0, 0.0).astype(jnp.bfloat16)
        for group in range(GROUPS):
            piece = jnp.dot(order, parts[step, group], preferred_element_type=jnp.float32)
            stage[step, :, group * span : (group + 1) * span] = piece[:, :span].astype(jnp.bfloat16)
        flying = []
        for d in range(1, 8):
            for half in range(2):
                origin = pl.ds(pl.multiple_of((z + d) % 8 * 32 + half * TILE, TILE), TILE)
                goal = pl.ds(pl.multiple_of(half * LANES + z * TILE, TILE), TILE)
                copy = remote(
                    stage.at[step, origin, :],
                    landing.at[step, goal, :],
                    row_send.at[step, d - 1, half],
                    row_recv.at[step, d - 1, half],
                    above[d - 1],
                )
                copy.start()
                flying.append(copy)
        for half in range(2):
            origin = pl.ds(pl.multiple_of(z * 32 + half * TILE, TILE), TILE)
            goal = pl.ds(pl.multiple_of(half * LANES + z * TILE, TILE), TILE)
            landing[step, goal, :] = stage[step, origin, :]
        return flying

    rows = 2 * LANES

    def temporal(step):
        hidden_in = jnp.dot(
            state[:, :PATCH].astype(jnp.bfloat16), embed_in[...], preferred_element_type=jnp.float32
        )
        out = jnp.dot(landing[step], shared[:, :width], preferred_element_type=jnp.float32)
        hidden = hidden_in + mods[0] * out
        normed = layer_norm(hidden) * (1.0 + mods[2]) + mods[1]
        triple[...] = jnp.dot(
            normed.astype(jnp.bfloat16),
            shared[:, width : 4 * width],
            preferred_element_type=jnp.float32,
        )

        def place_of(index):
            frame = index // SUB * 2 + index % 2
            return (frame + WIN - offsets[step]) // WIN * SUB + index % SUB // 2

        same = place_of(lax.broadcasted_iota(jnp.int32, (rows, 1), 0)) == place_of(
            lax.broadcasted_iota(jnp.int32, (1, rows), 1)
        )
        ones = one_column(rows)
        for head in range(HEADS):
            query = triple[:, head * HEAD : (head + 1) * HEAD]
            key = triple[:, width + head * HEAD : width + (head + 1) * HEAD]
            value = triple[:, 2 * width + head * HEAD : 2 * width + (head + 1) * HEAD]
            query = (query * (head_scale(query) * SHARPEN)).astype(jnp.bfloat16)
            key = (key * head_scale(key)).astype(jnp.bfloat16)
            value = jnp.concatenate([value.astype(jnp.bfloat16), ones], -1)
            raised = jnp.where(same, jnp.exp2(contract_last(query, key)), 0.0)
            part = jnp.dot(raised.astype(jnp.bfloat16), value, preferred_element_type=jnp.float32)
            part = part[:, :HEAD] / part[:, HEAD : HEAD + 1]
            mix[:, head * HEAD : (head + 1) * HEAD] = part.astype(jnp.bfloat16)
        out = jnp.dot(mix[...], shared[:, 4 * width :], preferred_element_type=jnp.float32)
        hidden = hidden + mods[3] * out
        velocity = jnp.dot(
            layer_norm(hidden).astype(jnp.bfloat16),
            embed_out[...],
            preferred_element_type=jnp.float32,
        )
        return state[:, :PATCH] + info[:, PATCH : PATCH + 1] * velocity, velocity

    pace = [1, 1, 1, 1, 1, 1, 1, 1]
    flying = spatial(0, shares, lambda: advance(pace.pop(0)))
    for copy in fact_copies:
        copy.wait()
    facts_rows = info[:, LANES:].astype(jnp.bfloat16)
    for part in range(4):
        columns = time_proj[:, (part + 2) * width : (part + 3) * width]
        mods[part] = jnp.dot(facts_rows, columns, preferred_element_type=jnp.float32)
    state[...] = info[:, :LANES]
    advance(len(plan))
    for kind in (1, 2):
        gather.collect(kind)
    restore_rows(blocks, shared, 8, 45, 12)
    for copy in flying:
        copy.wait()
    stepped, velocity = temporal(0)
    outgoing[...] = jnp.zeros((STEPS, rows, LANES), jnp.float32)
    outgoing[0, :, :PATCH] = stepped
    wide = outgoing[0]
    index = lax.broadcasted_iota(jnp.int32, (rows, LANES), 0)
    first = index % 2 == 0
    ahead = jnp.where(first, pltpu.roll(wide, rows - 1, 0), pltpu.roll(wide, rows - 7, 0))
    added = jnp.concatenate([fresh[...]] * (rows // SUB), 0)
    ahead = jnp.where(first | (index < rows - SUB), ahead, added)
    outgoing[0] = ahead
    flying = swap_rows(outgoing.at[0], back.at[0], swap_send.at[0], swap_recv.at[0])
    state[:, :PATCH] = ahead[:, :PATCH]
    state[:, PATCH : 2 * PATCH] = velocity
    target = lax.broadcasted_iota(jnp.int32, (LANES, rows), 0)
    source = lax.broadcasted_iota(jnp.int32, (LANES, rows), 1)
    moved = target // 64 * 16 + target % 32 // 4 * 2 + target // 32 % 2
    moved = moved * SUB + target % 4 * 2
    for copy in flying:
        copy.wait()
    arrived = back[0].astype(jnp.bfloat16)
    for j in range(2):
        order = jnp.where(moved + j == source, 1.0, 0.0).astype(jnp.bfloat16)
        piece = jnp.dot(order, arrived, preferred_element_type=jnp.float32)
        again[j] = piece.astype(jnp.bfloat16)
    shares = share(1, again)
    for copy in gather.started:
        copy.wait_send()
    for copy in spatial(1, shares, lambda: None):
        copy.wait()
    stepped, velocity = temporal(1)
    outgoing[1, :, :PATCH] = stepped
    outgoing[1, :, PATCH : 2 * PATCH] = state[:, PATCH : 2 * PATCH]
    outgoing[1, :, 2 * PATCH : 3 * PATCH] = velocity
    for copy in swap_rows(outgoing.at[1], back.at[1], swap_send.at[1], swap_recv.at[1]):
        copy.wait()
    for j in range(2):
        piece = back[1, pl.ds(j, LANES, stride=2), :]
        queue[j] = piece[:, :PATCH]
        velocities[0, j] = piece[:, PATCH : 2 * PATCH]
        velocities[1, j] = piece[:, 2 * PATCH : 3 * PATCH]


def network(offsets, *arrays):
    width, local_heads, rows = HEADS * HEAD, HEADS // GROUPS, 2 * LANES
    vmem = pl.BlockSpec(memory_space=pltpu.VMEM)
    shape = (2, LANES, PATCH)
    bf16, f32, dma = jnp.bfloat16, jnp.float32, pltpu.SemaphoreType.DMA
    return pl.pallas_call(
        network_kernel,
        out_shape=[
            jax.ShapeDtypeStruct(shape, f32),
            jax.ShapeDtypeStruct((STEPS, *shape), f32),
        ],
        in_specs=[pl.BlockSpec(memory_space=pltpu.SMEM)] + [vmem] * len(arrays),
        out_specs=[vmem] * 2,
        scratch_shapes=[
            pltpu.VMEM((32, CHUNKS[-1][1], TOP, LANES), bf16),
            pltpu.VMEM((SUB, 48 * LANES), f32),
            pltpu.VMEM((width, 7 * LANES), bf16),
            pltpu.VMEM((width, 5 * width), bf16),
            pltpu.VMEM((rows, 3 * LANES), f32),
            pltpu.VMEM((4, rows, width), f32),
            pltpu.VMEM((STEPS, 8 * LANES, LANES), bf16),
            pltpu.VMEM((STEPS, 8 * LANES, 3 * LANES), bf16),
            pltpu.VMEM((STEPS, GROUPS, rows, 3 * LANES), bf16),
            pltpu.VMEM((STEPS, rows, width), bf16),
            pltpu.VMEM((STEPS, rows, width), bf16),
            pltpu.VMEM((rows, LANES), f32),
            pltpu.VMEM((STEPS, rows, LANES), f32),
            pltpu.VMEM((STEPS, rows, LANES), f32),
            pltpu.VMEM((2, LANES, LANES), bf16),
            pltpu.VMEM((rows, 3 * width), f32),
            pltpu.VMEM((local_heads, 8 * LANES, HEAD), bf16),
            pltpu.VMEM((local_heads, 8 * LANES, HEAD), bf16),
            pltpu.VMEM((local_heads, 8 * LANES, LANES), bf16),
            pltpu.VMEM((rows, width), bf16),
            dma((40, 3)), dma((40, 3)), dma((31,)), dma((31,)), dma((STEPS, 7)), dma((STEPS, 7)),
            dma((STEPS, 31)), dma((STEPS, 31)), dma((STEPS, 7, 2)), dma((STEPS, 7, 2)),
            dma((STEPS, 31)), dma((STEPS, 31)),
        ],
        compiler_params=pltpu.CompilerParams(
            collective_id=0, has_side_effects=True, vmem_limit_bytes=VMEM_BYTES
        ),
        name="network",
    )(offsets, *arrays)


def row_facts(latents, step_size, features):
    count, tokens, size = latents.shape
    rows = latents.reshape(count, 32, tokens // 32, size)
    rows = jnp.transpose(rows, (1, 2, 0, 3)).reshape(2 * tokens, size)
    steps = jnp.broadcast_to(step_size[None], (tokens, count)).reshape(2 * tokens, 1)
    wide = jnp.broadcast_to(features.astype(jnp.float32)[None], (tokens, count, 2 * LANES))
    gap = jnp.zeros((2 * tokens, LANES - size - 1), jnp.float32)
    return jnp.concatenate([rows, steps, gap, wide.reshape(2 * tokens, 2 * LANES)], -1)


def plane_rows(latents):
    rows = latents.astype(jnp.bfloat16).reshape(2, 2, 8, 2, 4, PATCH)
    rows = jnp.swapaxes(rows, 2, 3).reshape(2, LANES, PATCH)
    return jnp.pad(rows, ((0, 0), (0, 0), (0, LANES - PATCH)))


def local(
    latents,
    fresh_noise,
    levels,
    timesteps,
    window_offsets,
    time_proj,
    embed_in,
    spatial_proj,
    spatial_out,
    temporal_proj,
    temporal_out,
    embed_out,
):
    which, row = lax.axis_index("space") % 2, lax.axis_index("frame")
    time_value = lookup_table(levels, timesteps)
    earlier = lookup_table(levels - 1, timesteps)
    features = time_features(time_value, time_proj.shape[0] // 2)
    facts = row_facts(latents, (earlier - time_value) / 1000.0, features)
    own = jnp.broadcast_to(lax.dynamic_index_in_dim(features, which, 0), (TILE, 2 * LANES))
    fresh = lax.dynamic_slice_in_dim(fresh_noise[0], row * 4, 4)
    fresh = jnp.pad(jnp.repeat(fresh, 2, axis=0), ((0, 0), (0, LANES - PATCH)))
    return network(
        window_offsets,
        plane_rows(latents),
        own,
        facts,
        fresh,
        time_proj,
        embed_in,
        embed_out,
        spatial_proj,
        spatial_out,
        temporal_proj,
        temporal_out,
    )


def solution(mesh):
    return jax.shard_map(
        local,
        mesh=mesh,
        in_specs=(
            P("frame", "space", None),
            P(None, "space", None),
            P("frame"),
            P(),
            P(),
            P(),
            P(),
            P("frame", None),
            P("frame", None),
            P("frame", None),
            P("frame", None),
            P(),
        ),
        out_specs=(P("frame", "space", None), P(None, "frame", "space", None)),
        check_vma=False,
    )
```

```python
import functools
import math

import jax
import jax.numpy as jnp
from jax import lax
from jax.experimental import pallas as pl
from jax.experimental.pallas import tpu as pltpu
from jax.sharding import PartitionSpec as P

HEADS = 16
HEAD = 72
WIN = 16
STEPS = 2
PATCH = 16
GROUPS = 4
LANES = 128
SUB = 8
TILE = 16
TOP = 32
MESH = pl.DeviceIdType.MESH
CHUNKS = ((0, 8), (8, 33), (33, 59))
HANDED, ACROSS = 16, 32
BLOCK = 256
SHARPEN = HEAD ** (-0.5) * math.log2(math.e)
VMEM_BYTES = 61 * 2**20


epsilon = 1e-06


def layer_norm(values):
    center = values - jnp.mean(values, -1, keepdims=True)
    spread = jnp.mean(center * center, -1, keepdims=True)
    return center * lax.rsqrt(spread + epsilon)


def lookup_table(indices, table):
    hits = indices[:, None] == jnp.arange(table.shape[0], dtype=jnp.int32)[None, :]
    return jnp.sum(jnp.where(hits, table[None, :], 0), axis=1).astype(jnp.float32)


def time_features(time_value, half):
    freqs = jnp.exp(-math.log(10000.0) * jnp.arange(half, dtype=jnp.float32) / half)
    angles = time_value[:, None] * freqs[None, :]
    return jnp.concatenate([jnp.cos(angles), jnp.sin(angles)], -1).astype(jnp.bfloat16)


def head_scale(values):
    return lax.rsqrt(jnp.mean(values * values, -1, keepdims=True) + epsilon)


def one_column(rows):
    lane = lax.broadcasted_iota(jnp.int32, (rows, LANES - HEAD), 1)
    return jnp.where(lane == 0, 1.0, 0.0).astype(jnp.bfloat16)


def contract_last(left, right):
    return lax.dot_general(
        left, right, (((1,), (1,)), ((), ())), preferred_element_type=jnp.float32
    )


def sites():
    frame, space = lax.axis_index("frame"), lax.axis_index("space")
    return frame // 16, frame // 2 % 8, frame % 2, space // 2, space % 2


def site_id(high, z, core, y, low):
    return {"frame": high * 16 + z * 2 + core, "space": y * 2 + low}


def greet(peers):
    barrier = pltpu.get_barrier_semaphore()
    for peer in peers:
        pl.semaphore_signal(barrier, inc=1, device_id=peer, device_id_type=MESH)
    return lambda: pl.semaphore_wait(barrier, len(peers))


def swap_rows(source, landing, send_sem, recv_sem):
    me, space = lax.axis_index("frame"), lax.axis_index("space")
    here = pl.ds(pl.multiple_of(me * SUB, SUB), SUB)
    flying = []
    for distance in range(1, 32):
        peer = (me + distance) % 32
        flying.append(
            remote(
                source.at[pl.ds(pl.multiple_of(peer * SUB, SUB), SUB), :],
                landing.at[here, :],
                send_sem.at[distance - 1],
                recv_sem.at[distance - 1],
                {"frame": peer, "space": space},
            )
        )
    landing[here, :] = source[here, :]
    return flying


def remote(source, target, send_sem, recv_sem, peer):
    return pltpu.make_async_remote_copy(
        src_ref=source,
        dst_ref=target,
        send_sem=send_sem,
        recv_sem=recv_sem,
        device_id=peer,
        device_id_type=MESH,
    )


def restore_order(quarter):
    row = lax.broadcasted_iota(jnp.int32, (144, 4 * TOP + 4 * TILE), 0)
    column = lax.broadcasted_iota(jnp.int32, (144, 4 * TOP + 4 * TILE), 1)
    device, inner = row // 36, row % 36
    source = jnp.where(
        inner < TOP, device * TOP + inner, 4 * TOP + device * TILE + quarter * 4 + inner - TOP
    )
    return jnp.where(source == column, 1.0, 0.0).astype(jnp.bfloat16)


class Gather:
    def __init__(self, blocks, send_sem, recv_sem):
        self.blocks, self.send_sem, self.recv_sem = blocks, send_sem, recv_sem
        high, z, core, y, low = sites()
        self.place = (high, z, core, y, low)
        self.up = site_id(high, (z + 1) % 8, core, y, low)
        self.down = site_id(high, (z + 7) % 8, core, y, low)
        self.across = site_id(1 - high, z, core, y, 1 - low)
        self.north = site_id(high, z, core, (y + 1) % 4, low)
        self.south = site_id(high, z, core, (y + 3) % 4, low)
        self.inner = site_id(high, z, core, y, 1 - low)
        self.sibling = site_id(high, z, 1 - core, y, low)
        self.mine = self.slot(high, z)
        self.handed = ([], [], [])
        self.passed = []
        self.started = []

    def slot(self, half, level):
        return half * 16 + level % 8 * 2 + self.place[2]

    def copy(self, kind, which, peer, index, half=None):
        first, last = CHUNKS[kind]
        if half is not None:
            middle = (first + last) // 2
            first, last = (first, middle) if half == 0 else (middle, last)
        piece = self.blocks.at[which, first:last]
        return remote(
            piece, piece, self.send_sem.at[index, kind], self.recv_sem.at[index, kind], peer
        )

    def send(self, kind, which, peer, index, half=None):
        copy = self.copy(kind, which, peer, index, half)
        copy.start()
        self.started.append(copy)

    def arrive(self, kind, which, peer, index, half=None):
        self.copy(kind, which, peer, index, half).wait_recv()

    def hand(self, kind, which):
        self.send(kind, which, self.sibling, HANDED + len(self.handed[kind]))
        self.handed[kind].append(which)

    def begin(self, kind):
        self.send(kind, self.mine, self.up, 0)
        self.send(kind, self.mine, self.down, 4)
        if kind == 0:
            self.pass_across(self.mine)
        self.hand(kind, self.mine)

    def pass_across(self, which):
        self.send(0, which, self.across, ACROSS + len(self.passed))
        self.passed.append(which)

    def hop(self, kind, hop):
        high, z, core, y, low = self.place
        half = (0, 1) if hop == 4 else (None, None)
        lower, upper = self.slot(high, z + 8 - hop), self.slot(high, z + hop)
        self.arrive(kind, lower, self.up, hop - 1, half[0])
        if hop < 4:
            self.send(kind, lower, self.up, hop, 0 if hop == 3 else None)
        self.arrive(kind, upper, self.down, 4 + hop - 1, half[1])
        if hop < 4:
            self.send(kind, upper, self.down, 4 + hop, 1 if hop == 3 else None)
        if kind == 0:
            for which in (lower, upper)[hop // 4 :]:
                self.pass_across(which)
        elif hop % 2 == 0:
            self.send(kind, self.brought(hop // 2 - 1, y, 1 - low, high), self.across, 7 + hop // 2)
        for which in (lower, upper)[hop // 4 :]:
            self.hand(kind, which)

    def finish_own(self, first, last):
        for index in range(first, last):
            which = self.passed[index]
            other = which + 16 - 32 * self.place[0]
            self.arrive(0, other, self.across, ACROSS + index)
            self.hand(0, other)

    def brought(self, far, y, low, half):
        return self.slot(half, self.place[1] + y % 2 * 2 + low + (3 if far else 7))

    def leg(self, kind, leg, far):
        high, z, core, y, low = self.place
        if leg == 0:
            which, index, peer = self.brought(far, y, low, 1 - high), 8, self.across
            onward = ((self.inner, 10), (self.north, 12))
        elif leg == 1:
            which, index, peer = self.brought(far, y, 1 - low, 1 - high), 10, self.inner
            onward = ((self.south, 14),)
        elif leg == 2:
            which, index, peer = self.brought(far, y + 1, low, 1 - high), 12, self.north
            onward = ()
        else:
            which, index, peer = self.brought(far, y + 1, 1 - low, 1 - high), 14, self.south
            onward = ()
        self.arrive(kind, which, peer, index + far)
        for target, number in onward:
            self.send(kind, which, target, number + far)
        self.hand(kind, which)

    def collect(self, kind):
        for index, which in enumerate(self.handed[kind]):
            self.arrive(kind, which + 1 - 2 * self.place[2], self.sibling, HANDED + index)

    def events(self):
        def hop(kind, number):
            return lambda: self.hop(kind, number)

        def leg(kind, number, far):
            return lambda: self.leg(kind, number, far)

        plan = [hop(1, 1), lambda: self.begin(2), hop(1, 2), hop(2, 1)]
        plan += [leg(1, 0, 0), hop(1, 3), hop(2, 2), leg(1, 1, 0), leg(1, 2, 0), hop(1, 4), hop(2, 3)]
        plan += [leg(2, 0, 0), hop(2, 4), leg(1, 3, 0), leg(2, 1, 0), leg(2, 2, 0), leg(1, 0, 1)]
        plan += [leg(2, 0, 1), leg(2, 3, 0), leg(1, 1, 1), leg(1, 2, 1), leg(2, 1, 1), leg(2, 2, 1)]
        plan += [leg(1, 3, 1), leg(2, 3, 1)]
        return plan


def pack_rows(blocks, mine, first, rest, tail, pieces):
    tile = 0
    for count, top, low in pieces:
        for number in range(count):
            blocks[mine, first + tile] = top(number)
            tail[0:4, tile * LANES : (tile + 1) * LANES] = low(number)
            tile += 1
    total = tail.shape[1] // LANES
    if total > tile:
        tail[0:4, tile * LANES :] = jnp.zeros((4, (total - tile) * LANES), jnp.float32)
    quarter = total // 4
    for number in range(quarter):
        rows = [
            tail[0:4, (a * quarter + number) * LANES : (a * quarter + number + 1) * LANES]
            for a in range(4)
        ]
        packed = jnp.concatenate(rows, 0).astype(jnp.bfloat16)
        blocks[mine, rest + number // 2, number % 2 * TILE : (number % 2 + 1) * TILE, :] = packed


def restore_rows(blocks, whole, first, rest, quarter, tiles):
    for a in range(4):
        start, stop = max(a * quarter, tiles[0]), min((a + 1) * quarter, tiles[1])
        if start >= stop:
            continue
        order = restore_order(a)

        @pl.loop(0, 8)
        def _(quad):
            four = pl.ds(quad * 4, 4)
            rows = pl.ds(pl.multiple_of(quad * 144, 16), 144)
            for begin in range(start, stop, 4):
                end = min(begin + 4, stop)
                columns = []
                for tile in range(begin, end):
                    number = tile - a * quarter
                    low = blocks[
                        four, rest + number // 2, number % 2 * TILE : (number % 2 + 1) * TILE, :
                    ]
                    top = blocks[four, first + tile]
                    columns.append(
                        jnp.concatenate(
                            [top.reshape(4 * TOP, LANES), low.reshape(4 * TILE, LANES)], 0
                        )
                    )
                joined = jnp.concatenate(columns, 1)
                result = jnp.dot(order, joined, preferred_element_type=jnp.float32)
                whole[rows, begin * LANES : end * LANES] = result.astype(jnp.bfloat16)


def network_kernel(
    offsets, latents, features, facts, fresh, time_proj, embed_in, embed_out,
    proj_s, out_s, proj_t, out_t, queue, velocities,
    blocks, tail, own, shared, info, mods, tokens, mixed, parts, stage, landing,
    state, outgoing, back, again, triple, qs, ks, vs, mix,
    gather_send, gather_recv, fact_send, fact_recv, share_send, share_recv,
    part_send, part_recv, row_send, row_recv, swap_send, swap_recv,
):
    high, z, core, y, low = sites()
    place, row = y * 2 + low, lax.axis_index("frame")
    width, local_heads = HEADS * HEAD, HEADS // GROUPS
    span = local_heads * HEAD

    def plane_peer(dy, a, b, c):
        return site_id((high + b) % 2, z, (core + c) % 2, (y + dy) % 4, (low + a) % 2)

    offs = [(dy, a, b, c) for dy in range(4) for a in range(2) for b in range(2) for c in range(2)]
    above = [site_id(high, (z + d) % 8, core, y, low) for d in range(1, 8)]
    frames = [(h, d, c) for h in range(2) for d in range(1, 8) for c in range(2)]
    everyone_here = greet(
        [plane_peer(*offset) for offset in offs[1:]]
        + [site_id((high + h) % 2, (z + d) % 8, (core + c) % 2, y, low) for h, d, c in frames]
    )

    mine = pl.ds(pl.multiple_of(place * LANES, LANES), LANES)
    near = [(dy, a) for dy in range(4) for a in range(2)]
    later = []

    def share(step, source):
        flying = [None]
        for index, (dy, a) in enumerate(near[1:]):
            other = (y + dy) % 4 * 2 + (low + a) % 2
            copy = remote(
                source.at[(low + a) % 2],
                tokens.at[step, mine, :],
                share_send.at[step, index],
                share_recv.at[step, index],
                {"frame": row, "space": other},
            )
            copy.start()
            flying.append(copy)
            later.append(copy)
        tokens[step, mine, :] = source[low]
        return flying

    gather = Gather(blocks, gather_send, gather_recv)
    source = lax.broadcasted_iota(jnp.int32, (width, span), 0)
    target = lax.broadcasted_iota(jnp.int32, (width, span), 1)
    chosen = jnp.where(source == target + y * span, 1.0, 0.0).astype(jnp.bfloat16)
    own_rows = triple
    for part in range(3):
        own_rows[0:36, part * span : (part + 1) * span] = jnp.dot(
            proj_s[:, part * width : (part + 1) * width], chosen, preferred_element_type=jnp.float32
        )
    own_rows[0:36, 3 * span : 7 * LANES] = jnp.zeros((36, 7 * LANES - 3 * span), jnp.float32)

    def wide_piece(number):
        return own_rows[0:TOP, number * LANES : (number + 1) * LANES].astype(jnp.bfloat16)

    def wide_rest(number):
        return own_rows[TOP:36, number * LANES : (number + 1) * LANES]

    pack_rows(blocks, gather.mine, 1, 0, tail.at[:, : 8 * LANES], [(7, wide_piece, wide_rest)])
    everyone_here()
    gather.begin(0)
    shares = share(0, latents)

    def pieces(ref):
        return (
            ref.shape[1] // LANES,
            lambda number: ref[:TOP, number * LANES : (number + 1) * LANES],
            lambda number: ref[TOP:, number * LANES : (number + 1) * LANES].astype(jnp.float32),
        )

    pack_rows(blocks, gather.mine, 14, 8, tail, [pieces(out_s), pieces(proj_t), pieces(out_t)])

    plan = gather.events()

    def advance(count):
        for _ in range(min(count, len(plan))):
            plan.pop(0)()

    gather.begin(1)
    gather.hop(0, 1)
    gather.hop(0, 2)
    advance(2)
    gather.hop(0, 3)
    gather.hop(0, 4)
    gather.finish_own(0, 5)
    advance(2)
    gather.finish_own(5, 8)
    gather.collect(0)
    restore_rows(blocks, own, 1, 0, 2, (0, 7))
    first_mods = jnp.dot(features[...], time_proj[:, : 2 * width], preferred_element_type=jnp.float32)
    shift, scale = first_mods[:1, :width], 1.0 + first_mods[:1, width:]
    mixed[:, :, span:] = jnp.zeros((STEPS, 8 * LANES, 3 * LANES - span), jnp.bfloat16)

    def spatial(step, shares, between):
        for dy in range(4):
            for a in range(2):
                if (dy, a) != (0, 0):
                    shares[near.index((-dy % 4, a))].wait_recv()
            here = pl.ds(pl.multiple_of((y + dy) % 4 * BLOCK, BLOCK), BLOCK)
            hidden = jnp.dot(
                tokens[step, here, :PATCH], embed_in[...], preferred_element_type=jnp.float32
            )
            normed = layer_norm(hidden) * scale + shift
            triple[:, : 7 * LANES] = jnp.dot(
                normed.astype(jnp.bfloat16), own[...], preferred_element_type=jnp.float32
            )
            for head in range(local_heads):
                query = triple[:, head * HEAD : (head + 1) * HEAD]
                key = triple[:, span + head * HEAD : span + (head + 1) * HEAD]
                value = triple[:, 2 * span + head * HEAD : 2 * span + (head + 1) * HEAD]
                qs[head, here, :] = (query * (head_scale(query) * SHARPEN)).astype(jnp.bfloat16)
                ks[head, here, :] = (key * head_scale(key)).astype(jnp.bfloat16)
                vs[head, here, :HEAD] = value.astype(jnp.bfloat16)
                vs[head, here, HEAD:] = one_column(BLOCK)
            between()
        sent = []
        own_part = pl.ds(pl.multiple_of((high * 4 + core * 2 + low) * 32, 32), 32)
        for dy in range(4):
            first = (y + dy) % 4 * BLOCK
            here = pl.ds(pl.multiple_of(first, BLOCK), BLOCK)
            for head in range(local_heads):
                raised = jnp.exp2(contract_last(qs[head, here, :], ks[head])).astype(jnp.bfloat16)
                part = jnp.dot(raised, vs[head], preferred_element_type=jnp.float32)
                part = part[:, :HEAD] / part[:, HEAD : HEAD + 1]
                mixed[step, here, head * HEAD : (head + 1) * HEAD] = part.astype(jnp.bfloat16)
            for index, (way, a, b, c) in enumerate(offs):
                if way != dy:
                    continue
                target = (low + a) % 2 * 4 + (high + b) % 2 * 2 + (core + c) % 2
                piece = pl.ds(pl.multiple_of(first + target * 32, 32), 32)
                if index == 0:
                    parts[step, y, own_part, :] = mixed[step, piece, :]
                    continue
                copy = remote(
                    mixed.at[step, piece, :],
                    parts.at[step, y, own_part, :],
                    part_send.at[step, index - 1],
                    part_recv.at[step, index - 1],
                    plane_peer(way, a, b, c),
                )
                copy.start()
                sent.append(copy)
            between()
        between()
        for copy in sent:
            copy.wait_recv()
        later.extend(sent)
        target = lax.broadcasted_iota(jnp.int32, (2 * LANES, 2 * LANES), 0)
        source = lax.broadcasted_iota(jnp.int32, (2 * LANES, 2 * LANES), 1)
        moved = target % 32 // 8 * 64 + target % 2 * 32 + target // 32 * 4 + target % 8 // 2
        order = jnp.where(moved == source, 1.0, 0.0).astype(jnp.bfloat16)
        for group in range(GROUPS):
            piece = jnp.dot(order, parts[step, group], preferred_element_type=jnp.float32)
            stage[step, :, group * span : (group + 1) * span] = piece[:, :span].astype(jnp.bfloat16)
        flying = []
        for d in range(1, 8):
            for half in range(2):
                origin = pl.ds(pl.multiple_of((z + d) % 8 * 32 + half * TILE, TILE), TILE)
                goal = pl.ds(pl.multiple_of(half * LANES + z * TILE, TILE), TILE)
                copy = remote(
                    stage.at[step, origin, :],
                    landing.at[step, goal, :],
                    row_send.at[step, d - 1, half],
                    row_recv.at[step, d - 1, half],
                    above[d - 1],
                )
                copy.start()
                flying.append(copy)
        for half in range(2):
            origin = pl.ds(pl.multiple_of(z * 32 + half * TILE, TILE), TILE)
            goal = pl.ds(pl.multiple_of(half * LANES + z * TILE, TILE), TILE)
            landing[step, goal, :] = stage[step, origin, :]
        later.extend(flying)
        return flying

    rows = 2 * LANES

    def temporal(step):
        hidden_in = jnp.dot(
            state[:, :PATCH].astype(jnp.bfloat16), embed_in[...], preferred_element_type=jnp.float32
        )
        out = jnp.dot(landing[step], shared[:, :width], preferred_element_type=jnp.float32)
        hidden = hidden_in + mods[0] * out
        normed = layer_norm(hidden) * (1.0 + mods[2]) + mods[1]
        triple[...] = jnp.dot(
            normed.astype(jnp.bfloat16),
            shared[:, width : 4 * width],
            preferred_element_type=jnp.float32,
        )

        def place_of(index):
            frame = index // SUB * 2 + index % 2
            return (frame + WIN - offsets[step]) // WIN * SUB + index % SUB // 2

        same = place_of(lax.broadcasted_iota(jnp.int32, (rows, 1), 0)) == place_of(
            lax.broadcasted_iota(jnp.int32, (1, rows), 1)
        )
        ones = one_column(rows)
        for head in range(HEADS):
            query = triple[:, head * HEAD : (head + 1) * HEAD]
            key = triple[:, width + head * HEAD : width + (head + 1) * HEAD]
            value = triple[:, 2 * width + head * HEAD : 2 * width + (head + 1) * HEAD]
            query = (query * (head_scale(query) * SHARPEN)).astype(jnp.bfloat16)
            key = (key * head_scale(key)).astype(jnp.bfloat16)
            value = jnp.concatenate([value.astype(jnp.bfloat16), ones], -1)
            raised = jnp.where(same, jnp.exp2(contract_last(query, key)), 0.0)
            part = jnp.dot(raised.astype(jnp.bfloat16), value, preferred_element_type=jnp.float32)
            part = part[:, :HEAD] / part[:, HEAD : HEAD + 1]
            mix[:, head * HEAD : (head + 1) * HEAD] = part.astype(jnp.bfloat16)
        out = jnp.dot(mix[...], shared[:, 4 * width :], preferred_element_type=jnp.float32)
        hidden = hidden + mods[3] * out
        velocity = contract_last(layer_norm(hidden).astype(jnp.bfloat16), embed_out[...])
        return state[:, :PATCH] + info[:, PATCH : PATCH + 1] * velocity, velocity

    pace = [1, 2, 1, 1, 2, 1, 1, 1, 2]
    fact_copies = swap_rows(facts, info, fact_send, fact_recv)
    waiting = list(fact_copies)

    def between():
        for _ in range(min(5, len(waiting))):
            waiting.pop(0).start()
        advance(pace.pop(0))

    flying = spatial(0, shares, between)
    for copy in fact_copies:
        copy.wait_recv()
    later.extend(fact_copies)
    facts_rows = info[:, LANES:].astype(jnp.bfloat16)
    for part in range(4):
        columns = time_proj[:, (part + 2) * width : (part + 3) * width]
        mods[part] = jnp.dot(facts_rows, columns, preferred_element_type=jnp.float32)
    state[...] = info[:, :LANES]
    advance(len(plan) - 1)
    gather.collect(1)
    restore_rows(blocks, shared, 14, 8, 12, (0, 19))
    advance(1)
    gather.collect(2)
    restore_rows(blocks, shared, 14, 8, 12, (19, 45))
    for copy in flying:
        copy.wait_recv()
    stepped, velocity = temporal(0)
    outgoing[...] = jnp.zeros((STEPS, rows, LANES), jnp.float32)
    outgoing[0, :, :PATCH] = stepped
    wide = outgoing[0]
    index = lax.broadcasted_iota(jnp.int32, (rows, LANES), 0)
    first = index % 2 == 0
    ahead = jnp.where(first, pltpu.roll(wide, rows - 1, 0), pltpu.roll(wide, rows - 7, 0))
    added = jnp.concatenate([fresh[...]] * (rows // SUB), 0)
    ahead = jnp.where(first | (index < rows - SUB), ahead, added)
    outgoing[0] = ahead
    flying = swap_rows(outgoing.at[0], back.at[0], swap_send.at[0], swap_recv.at[0])
    for copy in flying:
        copy.start()
    later.extend(flying)
    state[:, :PATCH] = ahead[:, :PATCH]
    state[:, PATCH : 2 * PATCH] = velocity
    target = lax.broadcasted_iota(jnp.int32, (LANES, rows), 0)
    source = lax.broadcasted_iota(jnp.int32, (LANES, rows), 1)
    moved = target // 64 * 16 + target % 32 // 4 * 2 + target // 32 % 2
    moved = moved * SUB + target % 4 * 2
    for copy in flying:
        copy.wait_recv()
    arrived = back[0].astype(jnp.bfloat16)
    for j in range(2):
        order = jnp.where(moved + j == source, 1.0, 0.0).astype(jnp.bfloat16)
        piece = jnp.dot(order, arrived, preferred_element_type=jnp.float32)
        again[j] = piece.astype(jnp.bfloat16)
    shares = share(1, again)
    flying = spatial(1, shares, lambda: None)
    for copy in gather.started + later:
        copy.wait_send()
    for copy in flying:
        copy.wait_recv()
    stepped, velocity = temporal(1)
    outgoing[1, :, :PATCH] = stepped
    outgoing[1, :, PATCH : 2 * PATCH] = state[:, PATCH : 2 * PATCH]
    outgoing[1, :, 2 * PATCH : 3 * PATCH] = velocity
    flying = swap_rows(outgoing.at[1], back.at[1], swap_send.at[1], swap_recv.at[1])
    for copy in flying:
        copy.start()
    for copy in flying:
        copy.wait()
    for j in range(2):
        piece = jnp.transpose(back[1, pl.ds(j, LANES, stride=2), :])
        queue[j] = piece[:PATCH]
        velocities[0, j] = piece[PATCH : 2 * PATCH]
        velocities[1, j] = piece[2 * PATCH : 3 * PATCH]


def network(offsets, *arrays):
    width, local_heads, rows = HEADS * HEAD, HEADS // GROUPS, 2 * LANES
    vmem = pl.BlockSpec(memory_space=pltpu.VMEM)
    shape = (2, PATCH, LANES)
    bf16, f32, dma = jnp.bfloat16, jnp.float32, pltpu.SemaphoreType.DMA
    return pl.pallas_call(
        network_kernel,
        out_shape=[
            jax.ShapeDtypeStruct(shape, f32),
            jax.ShapeDtypeStruct((STEPS, *shape), f32),
        ],
        in_specs=[pl.BlockSpec(memory_space=pltpu.SMEM)] + [vmem] * len(arrays),
        out_specs=[vmem] * 2,
        scratch_shapes=[
            pltpu.VMEM((32, CHUNKS[-1][1], TOP, LANES), bf16),
            pltpu.VMEM((SUB, 48 * LANES), f32),
            pltpu.VMEM((width, 7 * LANES), bf16),
            pltpu.VMEM((width, 5 * width), bf16),
            pltpu.VMEM((rows, 3 * LANES), f32),
            pltpu.VMEM((4, rows, width), f32),
            pltpu.VMEM((STEPS, 8 * LANES, LANES), bf16),
            pltpu.VMEM((STEPS, 8 * LANES, 3 * LANES), bf16),
            pltpu.VMEM((STEPS, GROUPS, rows, 3 * LANES), bf16),
            pltpu.VMEM((STEPS, rows, width), bf16),
            pltpu.VMEM((STEPS, rows, width), bf16),
            pltpu.VMEM((rows, LANES), f32),
            pltpu.VMEM((STEPS, rows, LANES), f32),
            pltpu.VMEM((STEPS, rows, LANES), f32),
            pltpu.VMEM((2, LANES, LANES), bf16),
            pltpu.VMEM((rows, 3 * width), f32),
            pltpu.VMEM((local_heads, 8 * LANES, HEAD), bf16),
            pltpu.VMEM((local_heads, 8 * LANES, HEAD), bf16),
            pltpu.VMEM((local_heads, 8 * LANES, LANES), bf16),
            pltpu.VMEM((rows, width), bf16),
            dma((40, 3)), dma((40, 3)), dma((31,)), dma((31,)), dma((STEPS, 7)), dma((STEPS, 7)),
            dma((STEPS, 31)), dma((STEPS, 31)), dma((STEPS, 7, 2)), dma((STEPS, 7, 2)),
            dma((STEPS, 31)), dma((STEPS, 31)),
        ],
        compiler_params=pltpu.CompilerParams(
            collective_id=0, has_side_effects=True, vmem_limit_bytes=VMEM_BYTES
        ),
        name="network",
    )(offsets, *arrays)


def row_facts(latents, step_size, features):
    count, tokens, size = latents.shape
    rows = latents.reshape(count, 32, tokens // 32, size)
    rows = jnp.transpose(rows, (1, 2, 0, 3)).reshape(2 * tokens, size)
    steps = jnp.broadcast_to(step_size[None], (tokens, count)).reshape(2 * tokens, 1)
    wide = jnp.broadcast_to(features.astype(jnp.float32)[None], (tokens, count, 2 * LANES))
    gap = jnp.zeros((2 * tokens, LANES - size - 1), jnp.float32)
    return jnp.concatenate([rows, steps, gap, wide.reshape(2 * tokens, 2 * LANES)], -1)


def plane_rows(latents):
    rows = latents.astype(jnp.bfloat16).reshape(2, 2, 8, 2, 4, PATCH)
    rows = jnp.swapaxes(rows, 2, 3).reshape(2, LANES, PATCH)
    return jnp.pad(rows, ((0, 0), (0, 0), (0, LANES - PATCH)))


def local(
    latents,
    fresh_noise,
    levels,
    timesteps,
    window_offsets,
    time_proj,
    embed_in,
    spatial_proj,
    spatial_out,
    temporal_proj,
    temporal_out,
    embed_out,
):
    which, row = lax.axis_index("space") % 2, lax.axis_index("frame")
    time_value = lookup_table(levels, timesteps)
    earlier = lookup_table(levels - 1, timesteps)
    features = time_features(time_value, time_proj.shape[0] // 2)
    facts = row_facts(latents, (earlier - time_value) / 1000.0, features)
    own = jnp.broadcast_to(lax.dynamic_index_in_dim(features, which, 0), (TILE, 2 * LANES))
    fresh = lax.dynamic_slice_in_dim(fresh_noise[0], row * 4, 4)
    fresh = jnp.pad(jnp.repeat(fresh, 2, axis=0), ((0, 0), (0, LANES - PATCH)))
    queue, velocities = network(
        window_offsets,
        plane_rows(latents),
        own,
        facts,
        fresh,
        time_proj,
        embed_in,
        embed_out.T,
        spatial_proj,
        spatial_out,
        temporal_proj,
        temporal_out,
    )
    return jnp.swapaxes(queue, 1, 2), jnp.swapaxes(velocities, 2, 3)


def solution(mesh):
    return jax.shard_map(
        local,
        mesh=mesh,
        in_specs=(
            P("frame", "space", None),
            P(None, "space", None),
            P("frame"),
            P(),
            P(),
            P(),
            P(),
            P("frame", None),
            P("frame", None),
            P("frame", None),
            P("frame", None),
            P(),
        ),
        out_specs=(P("frame", "space", None), P(None, "frame", "space", None)),
        check_vma=False,
    )
```

```python
import functools
import math

import jax
import jax.numpy as jnp
from jax import lax
from jax.experimental import pallas as pl
from jax.experimental.pallas import tpu as pltpu
from jax.sharding import PartitionSpec as P

HEADS = 16
HEAD = 72
WIN = 16
STEPS = 2
PATCH = 16
GROUPS = 4
LANES = 128
SUB = 8
TILE = 16
TOP = 32
MESH = pl.DeviceIdType.MESH
CHUNKS = ((0, 8), (8, 33), (33, 59))
HANDED, ACROSS = 16, 32
BLOCK = 256
SHARPEN = HEAD ** (-0.5) * math.log2(math.e)
VMEM_BYTES = 61 * 2**20


epsilon = 1e-06


def layer_norm(values):
    center = values - jnp.mean(values, -1, keepdims=True)
    spread = jnp.mean(center * center, -1, keepdims=True)
    return center * lax.rsqrt(spread + epsilon)


def lookup_table(indices, table):
    hits = indices[:, None] == jnp.arange(table.shape[0], dtype=jnp.int32)[None, :]
    return jnp.sum(jnp.where(hits, table[None, :], 0), axis=1).astype(jnp.float32)


def time_features(time_value, half):
    freqs = jnp.exp(-math.log(10000.0) * jnp.arange(half, dtype=jnp.float32) / half)
    angles = time_value[:, None] * freqs[None, :]
    return jnp.concatenate([jnp.cos(angles), jnp.sin(angles)], -1).astype(jnp.bfloat16)


def head_scale(values):
    return lax.rsqrt(jnp.mean(values * values, -1, keepdims=True) + epsilon)


def one_column(rows):
    lane = lax.broadcasted_iota(jnp.int32, (rows, LANES - HEAD), 1)
    return jnp.where(lane == 0, 1.0, 0.0).astype(jnp.bfloat16)


def contract_last(left, right):
    return lax.dot_general(
        left, right, (((1,), (1,)), ((), ())), preferred_element_type=jnp.float32
    )


def sites():
    frame, space = lax.axis_index("frame"), lax.axis_index("space")
    return frame // 16, frame // 2 % 8, frame % 2, space // 2, space % 2


def site_id(high, z, core, y, low):
    return {"frame": high * 16 + z * 2 + core, "space": y * 2 + low}


def greet(peers):
    barrier = pltpu.get_barrier_semaphore()
    for peer in peers:
        pl.semaphore_signal(barrier, inc=1, device_id=peer, device_id_type=MESH)
    return lambda: pl.semaphore_wait(barrier, len(peers))


def swap_rows(source, landing, send_sem, recv_sem):
    me, space = lax.axis_index("frame"), lax.axis_index("space")
    here = pl.ds(pl.multiple_of(me * SUB, SUB), SUB)
    flying = []
    for distance in range(1, 32):
        peer = (me + distance) % 32
        flying.append(
            remote(
                source.at[pl.ds(pl.multiple_of(peer * SUB, SUB), SUB), :],
                landing.at[here, :],
                send_sem.at[distance - 1],
                recv_sem.at[distance - 1],
                {"frame": peer, "space": space},
            )
        )
    landing[here, :] = source[here, :]
    return flying


def remote(source, target, send_sem, recv_sem, peer):
    return pltpu.make_async_remote_copy(
        src_ref=source,
        dst_ref=target,
        send_sem=send_sem,
        recv_sem=recv_sem,
        device_id=peer,
        device_id_type=MESH,
    )


class Gather:
    def __init__(self, blocks, send_sem, recv_sem):
        self.blocks, self.send_sem, self.recv_sem = blocks, send_sem, recv_sem
        high, z, core, y, low = sites()
        self.place = (high, z, core, y, low)
        self.up = site_id(high, (z + 1) % 8, core, y, low)
        self.down = site_id(high, (z + 7) % 8, core, y, low)
        self.across = site_id(1 - high, z, core, y, 1 - low)
        self.north = site_id(high, z, core, (y + 1) % 4, low)
        self.south = site_id(high, z, core, (y + 3) % 4, low)
        self.inner = site_id(high, z, core, y, 1 - low)
        self.sibling = site_id(high, z, 1 - core, y, low)
        self.mine = self.slot(high, z)
        self.handed = ([], [], [])
        self.passed = []
        self.started = []

    def slot(self, half, level):
        return half * 16 + level % 8 * 2 + self.place[2]

    def copy(self, kind, which, peer, index, half=None):
        first, last = CHUNKS[kind]
        if half is not None:
            middle = (first + last) // 2
            first, last = (first, middle) if half == 0 else (middle, last)
        piece = self.blocks.at[which, first:last]
        return remote(
            piece, piece, self.send_sem.at[index, kind], self.recv_sem.at[index, kind], peer
        )

    def send(self, kind, which, peer, index, half=None):
        copy = self.copy(kind, which, peer, index, half)
        copy.start()
        self.started.append(copy)

    def arrive(self, kind, which, peer, index, half=None):
        self.copy(kind, which, peer, index, half).wait_recv()

    def hand(self, kind, which):
        self.send(kind, which, self.sibling, HANDED + len(self.handed[kind]))
        self.handed[kind].append(which)

    def begin(self, kind):
        self.send(kind, self.mine, self.up, 0)
        self.send(kind, self.mine, self.down, 4)
        if kind == 0:
            self.pass_across(self.mine)
        self.hand(kind, self.mine)

    def pass_across(self, which):
        self.send(0, which, self.across, ACROSS + len(self.passed))
        self.passed.append(which)

    def hop(self, kind, hop):
        high, z, core, y, low = self.place
        half = (0, 1) if hop == 4 else (None, None)
        lower, upper = self.slot(high, z + 8 - hop), self.slot(high, z + hop)
        self.arrive(kind, lower, self.up, hop - 1, half[0])
        if hop < 4:
            self.send(kind, lower, self.up, hop, 0 if hop == 3 else None)
        self.arrive(kind, upper, self.down, 4 + hop - 1, half[1])
        if hop < 4:
            self.send(kind, upper, self.down, 4 + hop, 1 if hop == 3 else None)
        if kind == 0:
            for which in (lower, upper)[hop // 4 :]:
                self.pass_across(which)
        elif hop % 2 == 0:
            self.send(kind, self.brought(hop // 2 - 1, y, 1 - low, high), self.across, 7 + hop // 2)
        for which in (lower, upper)[hop // 4 :]:
            self.hand(kind, which)

    def finish_own(self, first, last):
        for index in range(first, last):
            which = self.passed[index]
            other = which + 16 - 32 * self.place[0]
            self.arrive(0, other, self.across, ACROSS + index)
            self.hand(0, other)

    def brought(self, far, y, low, half):
        return self.slot(half, self.place[1] + y % 2 * 2 + low + (3 if far else 7))

    def leg(self, kind, leg, far):
        high, z, core, y, low = self.place
        if leg == 0:
            which, index, peer = self.brought(far, y, low, 1 - high), 8, self.across
            onward = ((self.inner, 10), (self.north, 12))
        elif leg == 1:
            which, index, peer = self.brought(far, y, 1 - low, 1 - high), 10, self.inner
            onward = ((self.south, 14),)
        elif leg == 2:
            which, index, peer = self.brought(far, y + 1, low, 1 - high), 12, self.north
            onward = ()
        else:
            which, index, peer = self.brought(far, y + 1, 1 - low, 1 - high), 14, self.south
            onward = ()
        self.arrive(kind, which, peer, index + far)
        for target, number in onward:
            self.send(kind, which, target, number + far)
        self.hand(kind, which)

    def collect(self, kind):
        for index, which in enumerate(self.handed[kind]):
            self.arrive(kind, which + 1 - 2 * self.place[2], self.sibling, HANDED + index)

    def events(self):
        def hop(kind, number):
            return lambda: self.hop(kind, number)

        def leg(kind, number, far):
            return lambda: self.leg(kind, number, far)

        plan = [hop(1, 1), lambda: self.begin(2), hop(1, 2), hop(2, 1)]
        plan += [leg(1, 0, 0), hop(1, 3), hop(2, 2), leg(1, 1, 0), leg(1, 2, 0), hop(1, 4), hop(2, 3)]
        plan += [leg(2, 0, 0), hop(2, 4), leg(1, 3, 0), leg(2, 1, 0), leg(2, 2, 0), leg(1, 0, 1)]
        plan += [leg(2, 0, 1), leg(2, 3, 0), leg(1, 1, 1), leg(1, 2, 1), leg(2, 1, 1), leg(2, 2, 1)]
        plan += [leg(1, 3, 1), leg(2, 3, 1)]
        return plan


def pack_rows(blocks, mine, first, rest, tail, pieces):
    tile = 0
    for count, top, low in pieces:
        for number in range(count):
            blocks[mine, first + tile] = top(number)
            tail[0:4, tile * LANES : (tile + 1) * LANES] = low(number)
            tile += 1
    total = tail.shape[1] // LANES
    if total > tile:
        tail[0:4, tile * LANES :] = jnp.zeros((4, (total - tile) * LANES), jnp.float32)
    quarter = total // 4
    for number in range(quarter):
        rows = [
            tail[0:4, (a * quarter + number) * LANES : (a * quarter + number + 1) * LANES]
            for a in range(4)
        ]
        packed = jnp.concatenate(rows, 0).astype(jnp.bfloat16)
        blocks[mine, rest + number // 2, number % 2 * TILE : (number % 2 + 1) * TILE, :] = packed


def restore_rows(blocks, whole, first, rest, quarter, tiles):
    @pl.loop(0, 8)
    def _(quad):
        rows = pl.ds(pl.multiple_of(quad * 144, 16), 144)
        for tile in range(*tiles):
            a, number = tile // quarter, tile % quarter
            half = number % 2 * TILE
            pieces = []
            for device in range(4):
                which = quad * 4 + device
                pieces.append(blocks[which, first + tile].astype(jnp.float32))
                low = blocks[which, rest + number // 2, half : half + TILE, :].astype(jnp.float32)
                pieces.append(low[a * 4 : a * 4 + 4])
            joined = jnp.concatenate(pieces, 0)
            whole[rows, tile * LANES : (tile + 1) * LANES] = joined.astype(jnp.bfloat16)


def network_kernel(
    offsets, latents, features, facts, fresh, time_proj, embed_in, embed_out,
    proj_s, out_s, proj_t, out_t, queue, velocities,
    blocks, tail, own, shared, info, mods, tokens, mixed, parts, stage, landing,
    state, outgoing, back, again, triple, qs, ks, vs, mix,
    gather_send, gather_recv, fact_send, fact_recv, share_send, share_recv,
    part_send, part_recv, row_send, row_recv, swap_send, swap_recv,
):
    high, z, core, y, low = sites()
    place, row = y * 2 + low, lax.axis_index("frame")
    width, local_heads = HEADS * HEAD, HEADS // GROUPS
    span = local_heads * HEAD

    def plane_peer(dy, a, b, c):
        return site_id((high + b) % 2, z, (core + c) % 2, (y + dy) % 4, (low + a) % 2)

    offs = [(dy, a, b, c) for dy in range(4) for a in range(2) for b in range(2) for c in range(2)]
    above = [site_id(high, (z + d) % 8, core, y, low) for d in range(1, 8)]
    frames = [(h, d, c) for h in range(2) for d in range(1, 8) for c in range(2)]
    everyone_here = greet(
        [plane_peer(*offset) for offset in offs[1:]]
        + [site_id((high + h) % 2, (z + d) % 8, (core + c) % 2, y, low) for h, d, c in frames]
    )

    mine = pl.ds(pl.multiple_of(place * LANES, LANES), LANES)
    near = [(dy, a) for dy in range(4) for a in range(2)]
    later = []

    def share(step, source):
        flying = [None]
        for index, (dy, a) in enumerate(near[1:]):
            other = (y + dy) % 4 * 2 + (low + a) % 2
            copy = remote(
                source.at[(low + a) % 2],
                tokens.at[step, mine, :],
                share_send.at[step, index],
                share_recv.at[step, index],
                {"frame": row, "space": other},
            )
            copy.start()
            flying.append(copy)
            later.append(copy)
        tokens[step, mine, :] = source[low]
        return flying

    gather = Gather(blocks, gather_send, gather_recv)
    source = lax.broadcasted_iota(jnp.int32, (width, span), 0)
    target = lax.broadcasted_iota(jnp.int32, (width, span), 1)
    chosen = jnp.where(source == target + y * span, 1.0, 0.0).astype(jnp.bfloat16)
    own_rows = triple
    for part in range(3):
        own_rows[0:36, part * span : (part + 1) * span] = jnp.dot(
            proj_s[:, part * width : (part + 1) * width], chosen, preferred_element_type=jnp.float32
        )
    own_rows[0:36, 3 * span : 7 * LANES] = jnp.zeros((36, 7 * LANES - 3 * span), jnp.float32)

    def wide_piece(number):
        return own_rows[0:TOP, number * LANES : (number + 1) * LANES].astype(jnp.bfloat16)

    def wide_rest(number):
        return own_rows[TOP:36, number * LANES : (number + 1) * LANES]

    pack_rows(blocks, gather.mine, 1, 0, tail.at[:, : 8 * LANES], [(7, wide_piece, wide_rest)])
    everyone_here()
    gather.begin(0)
    shares = share(0, latents)

    def pieces(ref):
        return (
            ref.shape[1] // LANES,
            lambda number: ref[:TOP, number * LANES : (number + 1) * LANES],
            lambda number: ref[TOP:, number * LANES : (number + 1) * LANES].astype(jnp.float32),
        )

    pack_rows(blocks, gather.mine, 14, 8, tail, [pieces(out_s), pieces(proj_t), pieces(out_t)])

    plan = gather.events()

    def advance(count):
        for _ in range(min(count, len(plan))):
            plan.pop(0)()

    gather.begin(1)
    gather.hop(0, 1)
    gather.hop(0, 2)
    advance(2)
    gather.hop(0, 3)
    gather.hop(0, 4)
    gather.finish_own(0, 5)
    advance(2)
    gather.finish_own(5, 8)
    gather.collect(0)
    restore_rows(blocks, own, 1, 0, 2, (0, 7))
    first_mods = jnp.dot(features[...], time_proj[:, : 2 * width], preferred_element_type=jnp.float32)
    shift, scale = first_mods[:1, :width], 1.0 + first_mods[:1, width:]
    mixed[:, :, span:] = jnp.zeros((STEPS, 8 * LANES, 3 * LANES - span), jnp.bfloat16)

    def spatial(step, shares, between):
        for dy in range(4):
            for a in range(2):
                if (dy, a) != (0, 0):
                    shares[near.index((-dy % 4, a))].wait_recv()
            here = pl.ds(pl.multiple_of((y + dy) % 4 * BLOCK, BLOCK), BLOCK)
            hidden = jnp.dot(
                tokens[step, here, :PATCH], embed_in[...], preferred_element_type=jnp.float32
            )
            normed = layer_norm(hidden) * scale + shift
            triple[:, : 7 * LANES] = jnp.dot(
                normed.astype(jnp.bfloat16), own[...], preferred_element_type=jnp.float32
            )
            for head in range(local_heads):
                query = triple[:, head * HEAD : (head + 1) * HEAD]
                key = triple[:, span + head * HEAD : span + (head + 1) * HEAD]
                value = triple[:, 2 * span + head * HEAD : 2 * span + (head + 1) * HEAD]
                qs[head, here, :] = (query * (head_scale(query) * SHARPEN)).astype(jnp.bfloat16)
                ks[head, here, :] = (key * head_scale(key)).astype(jnp.bfloat16)
                vs[head, here, :HEAD] = value.astype(jnp.bfloat16)
                vs[head, here, HEAD:] = one_column(BLOCK)
            between()
        sent = []
        own_part = pl.ds(pl.multiple_of((high * 4 + core * 2 + low) * 32, 32), 32)
        for dy in range(4):
            first = (y + dy) % 4 * BLOCK
            here = pl.ds(pl.multiple_of(first, BLOCK), BLOCK)
            for head in range(local_heads):
                raised = jnp.exp2(contract_last(qs[head, here, :], ks[head])).astype(jnp.bfloat16)
                part = jnp.dot(raised, vs[head], preferred_element_type=jnp.float32)
                part = part[:, :HEAD] / part[:, HEAD : HEAD + 1]
                mixed[step, here, head * HEAD : (head + 1) * HEAD] = part.astype(jnp.bfloat16)
            for index, (way, a, b, c) in enumerate(offs):
                if way != dy:
                    continue
                target = (low + a) % 2 * 4 + (high + b) % 2 * 2 + (core + c) % 2
                piece = pl.ds(pl.multiple_of(first + target * 32, 32), 32)
                if index == 0:
                    parts[step, y, own_part, :] = mixed[step, piece, :]
                    continue
                copy = remote(
                    mixed.at[step, piece, :],
                    parts.at[step, y, own_part, :],
                    part_send.at[step, index - 1],
                    part_recv.at[step, index - 1],
                    plane_peer(way, a, b, c),
                )
                copy.start()
                sent.append(copy)
            between()
        between()
        for copy in sent:
            copy.wait_recv()
        later.extend(sent)
        target = lax.broadcasted_iota(jnp.int32, (2 * LANES, 2 * LANES), 0)
        source = lax.broadcasted_iota(jnp.int32, (2 * LANES, 2 * LANES), 1)
        moved = target % 32 // 8 * 64 + target % 2 * 32 + target // 32 * 4 + target % 8 // 2
        order = jnp.where(moved == source, 1.0, 0.0).astype(jnp.bfloat16)
        for group in range(GROUPS):
            piece = jnp.dot(order, parts[step, group], preferred_element_type=jnp.float32)
            stage[step, :, group * span : (group + 1) * span] = piece[:, :span].astype(jnp.bfloat16)
        flying = []
        for d in range(1, 8):
            for half in range(2):
                origin = pl.ds(pl.multiple_of((z + d) % 8 * 32 + half * TILE, TILE), TILE)
                goal = pl.ds(pl.multiple_of(half * LANES + z * TILE, TILE), TILE)
                copy = remote(
                    stage.at[step, origin, :],
                    landing.at[step, goal, :],
                    row_send.at[step, d - 1, half],
                    row_recv.at[step, d - 1, half],
                    above[d - 1],
                )
                copy.start()
                flying.append(copy)
        for half in range(2):
            origin = pl.ds(pl.multiple_of(z * 32 + half * TILE, TILE), TILE)
            goal = pl.ds(pl.multiple_of(half * LANES + z * TILE, TILE), TILE)
            landing[step, goal, :] = stage[step, origin, :]
        later.extend(flying)
        return flying

    rows = 2 * LANES

    def temporal_head(step):
        hidden_in = jnp.dot(
            state[:, :PATCH].astype(jnp.bfloat16), embed_in[...], preferred_element_type=jnp.float32
        )
        out = jnp.dot(landing[step], shared[:, :width], preferred_element_type=jnp.float32)
        hidden = hidden_in + mods[0] * out
        normed = layer_norm(hidden) * (1.0 + mods[2]) + mods[1]
        mix[...] = normed.astype(jnp.bfloat16)
        return hidden

    def temporal(step, hidden):
        triple[...] = jnp.dot(
            mix[...], shared[:, width : 4 * width], preferred_element_type=jnp.float32
        )

        def place_of(index):
            frame = index // SUB * 2 + index % 2
            return (frame + WIN - offsets[step]) // WIN * SUB + index % SUB // 2

        same = place_of(lax.broadcasted_iota(jnp.int32, (rows, 1), 0)) == place_of(
            lax.broadcasted_iota(jnp.int32, (1, rows), 1)
        )
        ones = one_column(rows)
        for head in range(HEADS):
            query = triple[:, head * HEAD : (head + 1) * HEAD]
            key = triple[:, width + head * HEAD : width + (head + 1) * HEAD]
            value = triple[:, 2 * width + head * HEAD : 2 * width + (head + 1) * HEAD]
            query = (query * (head_scale(query) * SHARPEN)).astype(jnp.bfloat16)
            key = (key * head_scale(key)).astype(jnp.bfloat16)
            value = jnp.concatenate([value.astype(jnp.bfloat16), ones], -1)
            raised = jnp.where(same, jnp.exp2(contract_last(query, key)), 0.0)
            part = jnp.dot(raised.astype(jnp.bfloat16), value, preferred_element_type=jnp.float32)
            part = part[:, :HEAD] / part[:, HEAD : HEAD + 1]
            mix[:, head * HEAD : (head + 1) * HEAD] = part.astype(jnp.bfloat16)
        out = jnp.dot(mix[...], shared[:, 4 * width :], preferred_element_type=jnp.float32)
        hidden = hidden + mods[3] * out
        velocity = contract_last(layer_norm(hidden).astype(jnp.bfloat16), embed_out[...])
        return state[:, :PATCH] + info[:, PATCH : PATCH + 1] * velocity, velocity

    pace = [1, 2, 1, 1, 2, 1, 1, 1, 2]
    fact_copies = swap_rows(facts, info, fact_send, fact_recv)
    waiting = list(fact_copies)

    def between():
        for _ in range(min(5, len(waiting))):
            waiting.pop(0).start()
        advance(pace.pop(0))

    flying = spatial(0, shares, between)
    for copy in fact_copies:
        copy.wait_recv()
    later.extend(fact_copies)
    facts_rows = info[:, LANES:].astype(jnp.bfloat16)
    for part in range(4):
        columns = time_proj[:, (part + 2) * width : (part + 3) * width]
        mods[part] = jnp.dot(facts_rows, columns, preferred_element_type=jnp.float32)
    state[...] = info[:, :LANES]
    advance(len(plan) - 1)
    gather.collect(1)
    restore_rows(blocks, shared, 14, 8, 12, (0, 19))
    for copy in flying:
        copy.wait_recv()
    hidden = temporal_head(0)
    advance(1)
    gather.collect(2)
    restore_rows(blocks, shared, 14, 8, 12, (19, 45))
    stepped, velocity = temporal(0, hidden)
    outgoing[...] = jnp.zeros((STEPS, rows, LANES), jnp.float32)
    outgoing[0, :, :PATCH] = stepped
    wide = outgoing[0]
    index = lax.broadcasted_iota(jnp.int32, (rows, LANES), 0)
    first = index % 2 == 0
    ahead = jnp.where(first, pltpu.roll(wide, rows - 1, 0), pltpu.roll(wide, rows - 7, 0))
    added = jnp.concatenate([fresh[...]] * (rows // SUB), 0)
    ahead = jnp.where(first | (index < rows - SUB), ahead, added)
    outgoing[0] = ahead
    flying = swap_rows(outgoing.at[0], back.at[0], swap_send.at[0], swap_recv.at[0])
    for copy in flying:
        copy.start()
    later.extend(flying)
    state[:, :PATCH] = ahead[:, :PATCH]
    state[:, PATCH : 2 * PATCH] = velocity
    target = lax.broadcasted_iota(jnp.int32, (LANES, rows), 0)
    source = lax.broadcasted_iota(jnp.int32, (LANES, rows), 1)
    moved = target // 64 * 16 + target % 32 // 4 * 2 + target // 32 % 2
    moved = moved * SUB + target % 4 * 2
    for copy in flying:
        copy.wait_recv()
    arrived = back[0].astype(jnp.bfloat16)
    for j in range(2):
        order = jnp.where(moved + j == source, 1.0, 0.0).astype(jnp.bfloat16)
        piece = jnp.dot(order, arrived, preferred_element_type=jnp.float32)
        again[j] = piece.astype(jnp.bfloat16)
    shares = share(1, again)
    flying = spatial(1, shares, lambda: None)
    for copy in gather.started + later:
        copy.wait_send()
    for copy in flying:
        copy.wait_recv()
    stepped, velocity = temporal(1, temporal_head(1))
    outgoing[1, :, :PATCH] = stepped
    outgoing[1, :, PATCH : 2 * PATCH] = state[:, PATCH : 2 * PATCH]
    outgoing[1, :, 2 * PATCH : 3 * PATCH] = velocity
    flying = swap_rows(outgoing.at[1], back.at[1], swap_send.at[1], swap_recv.at[1])
    for copy in flying:
        copy.start()
    for copy in flying:
        copy.wait()
    for j in range(2):
        piece = jnp.transpose(back[1, pl.ds(j, LANES, stride=2), :])
        queue[j] = piece[:PATCH]
        velocities[0, j] = piece[PATCH : 2 * PATCH]
        velocities[1, j] = piece[2 * PATCH : 3 * PATCH]


def network(offsets, *arrays):
    width, local_heads, rows = HEADS * HEAD, HEADS // GROUPS, 2 * LANES
    vmem = pl.BlockSpec(memory_space=pltpu.VMEM)
    shape = (2, PATCH, LANES)
    bf16, f32, dma = jnp.bfloat16, jnp.float32, pltpu.SemaphoreType.DMA
    return pl.pallas_call(
        network_kernel,
        out_shape=[
            jax.ShapeDtypeStruct(shape, f32),
            jax.ShapeDtypeStruct((STEPS, *shape), f32),
        ],
        in_specs=[pl.BlockSpec(memory_space=pltpu.SMEM)] + [vmem] * len(arrays),
        out_specs=[vmem] * 2,
        scratch_shapes=[
            pltpu.VMEM((32, CHUNKS[-1][1], TOP, LANES), bf16),
            pltpu.VMEM((SUB, 48 * LANES), f32),
            pltpu.VMEM((width, 7 * LANES), bf16),
            pltpu.VMEM((width, 5 * width), bf16),
            pltpu.VMEM((rows, 3 * LANES), f32),
            pltpu.VMEM((4, rows, width), f32),
            pltpu.VMEM((STEPS, 8 * LANES, LANES), bf16),
            pltpu.VMEM((STEPS, 8 * LANES, 3 * LANES), bf16),
            pltpu.VMEM((STEPS, GROUPS, rows, 3 * LANES), bf16),
            pltpu.VMEM((STEPS, rows, width), bf16),
            pltpu.VMEM((STEPS, rows, width), bf16),
            pltpu.VMEM((rows, LANES), f32),
            pltpu.VMEM((STEPS, rows, LANES), f32),
            pltpu.VMEM((STEPS, rows, LANES), f32),
            pltpu.VMEM((2, LANES, LANES), bf16),
            pltpu.VMEM((rows, 3 * width), f32),
            pltpu.VMEM((local_heads, 8 * LANES, HEAD), bf16),
            pltpu.VMEM((local_heads, 8 * LANES, HEAD), bf16),
            pltpu.VMEM((local_heads, 8 * LANES, LANES), bf16),
            pltpu.VMEM((rows, width), bf16),
            dma((40, 3)), dma((40, 3)), dma((31,)), dma((31,)), dma((STEPS, 7)), dma((STEPS, 7)),
            dma((STEPS, 31)), dma((STEPS, 31)), dma((STEPS, 7, 2)), dma((STEPS, 7, 2)),
            dma((STEPS, 31)), dma((STEPS, 31)),
        ],
        compiler_params=pltpu.CompilerParams(
            collective_id=0, has_side_effects=True, vmem_limit_bytes=VMEM_BYTES
        ),
        name="network",
    )(offsets, *arrays)


def row_facts(latents, step_size, features):
    count, tokens, size = latents.shape
    rows = latents.reshape(count, 32, tokens // 32, size)
    rows = jnp.transpose(rows, (1, 2, 0, 3)).reshape(2 * tokens, size)
    steps = jnp.broadcast_to(step_size[None], (tokens, count)).reshape(2 * tokens, 1)
    wide = jnp.broadcast_to(features.astype(jnp.float32)[None], (tokens, count, 2 * LANES))
    gap = jnp.zeros((2 * tokens, LANES - size - 1), jnp.float32)
    return jnp.concatenate([rows, steps, gap, wide.reshape(2 * tokens, 2 * LANES)], -1)


def plane_rows(latents):
    rows = latents.astype(jnp.bfloat16).reshape(2, 2, 8, 2, 4, PATCH)
    rows = jnp.swapaxes(rows, 2, 3).reshape(2, LANES, PATCH)
    return jnp.pad(rows, ((0, 0), (0, 0), (0, LANES - PATCH)))


def local(
    latents,
    fresh_noise,
    levels,
    timesteps,
    window_offsets,
    time_proj,
    embed_in,
    spatial_proj,
    spatial_out,
    temporal_proj,
    temporal_out,
    embed_out,
):
    which, row = lax.axis_index("space") % 2, lax.axis_index("frame")
    time_value = lookup_table(levels, timesteps)
    earlier = lookup_table(levels - 1, timesteps)
    features = time_features(time_value, time_proj.shape[0] // 2)
    facts = row_facts(latents, (earlier - time_value) / 1000.0, features)
    own = jnp.broadcast_to(lax.dynamic_index_in_dim(features, which, 0), (TILE, 2 * LANES))
    fresh = lax.dynamic_slice_in_dim(fresh_noise[0], row * 4, 4)
    fresh = jnp.pad(jnp.repeat(fresh, 2, axis=0), ((0, 0), (0, LANES - PATCH)))
    queue, velocities = network(
        window_offsets,
        plane_rows(latents),
        own,
        facts,
        fresh,
        time_proj,
        embed_in,
        embed_out.T,
        spatial_proj,
        spatial_out,
        temporal_proj,
        temporal_out,
    )
    return jnp.swapaxes(queue, 1, 2), jnp.swapaxes(velocities, 2, 3)


def solution(mesh):
    return jax.shard_map(
        local,
        mesh=mesh,
        in_specs=(
            P("frame", "space", None),
            P(None, "space", None),
            P("frame"),
            P(),
            P(),
            P(),
            P(),
            P("frame", None),
            P("frame", None),
            P("frame", None),
            P("frame", None),
            P(),
        ),
        out_specs=(P("frame", "space", None), P(None, "frame", "space", None)),
        check_vma=False,
    )
```

```python
import functools
import math

import jax
import jax.numpy as jnp
from jax import lax
from jax.experimental import pallas as pl
from jax.experimental.pallas import tpu as pltpu
from jax.sharding import PartitionSpec as P

HEADS = 16
HEAD = 72
WIN = 16
STEPS = 2
PATCH = 16
GROUPS = 4
LANES = 128
SUB = 8
TILE = 16
TOP = 32
MESH = pl.DeviceIdType.MESH
CHUNKS = ((0, 8), (8, 33), (33, 59))
HANDED, ACROSS = 16, 32
BLOCK = 256
SHARPEN = HEAD ** (-0.5) * math.log2(math.e)
VMEM_BYTES = 61 * 2**20


epsilon = 1e-06


def layer_norm(values):
    center = values - jnp.mean(values, -1, keepdims=True)
    spread = jnp.mean(center * center, -1, keepdims=True)
    return center * lax.rsqrt(spread + epsilon)


def lookup_table(indices, table):
    hits = indices[:, None] == jnp.arange(table.shape[0], dtype=jnp.int32)[None, :]
    return jnp.sum(jnp.where(hits, table[None, :], 0), axis=1).astype(jnp.float32)


def time_features(time_value, half):
    freqs = jnp.exp(-math.log(10000.0) * jnp.arange(half, dtype=jnp.float32) / half)
    angles = time_value[:, None] * freqs[None, :]
    return jnp.concatenate([jnp.cos(angles), jnp.sin(angles)], -1).astype(jnp.bfloat16)


def head_scale(values):
    return lax.rsqrt(jnp.mean(values * values, -1, keepdims=True) + epsilon)


def one_column(rows):
    lane = lax.broadcasted_iota(jnp.int32, (rows, LANES - HEAD), 1)
    return jnp.where(lane == 0, 1.0, 0.0).astype(jnp.bfloat16)


def contract_last(left, right):
    return lax.dot_general(
        left, right, (((1,), (1,)), ((), ())), preferred_element_type=jnp.float32
    )


def sites():
    frame, space = lax.axis_index("frame"), lax.axis_index("space")
    return frame // 16, frame // 2 % 8, frame % 2, space // 2, space % 2


def site_id(high, z, core, y, low):
    return {"frame": high * 16 + z * 2 + core, "space": y * 2 + low}


def greet(peers):
    barrier = pltpu.get_barrier_semaphore()
    for peer in peers:
        pl.semaphore_signal(barrier, inc=1, device_id=peer, device_id_type=MESH)
    return lambda: pl.semaphore_wait(barrier, len(peers))


def swap_rows(source, landing, send_sem, recv_sem):
    me, space = lax.axis_index("frame"), lax.axis_index("space")
    here = pl.ds(pl.multiple_of(me * SUB, SUB), SUB)
    flying = []
    for distance in range(1, 32):
        peer = (me + distance) % 32
        flying.append(
            remote(
                source.at[pl.ds(pl.multiple_of(peer * SUB, SUB), SUB), :],
                landing.at[here, :],
                send_sem.at[distance - 1],
                recv_sem.at[distance - 1],
                {"frame": peer, "space": space},
            )
        )
    landing[here, :] = source[here, :]
    return flying


def remote(source, target, send_sem, recv_sem, peer):
    return pltpu.make_async_remote_copy(
        src_ref=source,
        dst_ref=target,
        send_sem=send_sem,
        recv_sem=recv_sem,
        device_id=peer,
        device_id_type=MESH,
    )


class Gather:
    def __init__(self, blocks, send_sem, recv_sem):
        self.blocks, self.send_sem, self.recv_sem = blocks, send_sem, recv_sem
        high, z, core, y, low = sites()
        self.place = (high, z, core, y, low)
        self.up = site_id(high, (z + 1) % 8, core, y, low)
        self.down = site_id(high, (z + 7) % 8, core, y, low)
        self.across = site_id(1 - high, z, core, y, 1 - low)
        self.north = site_id(high, z, core, (y + 1) % 4, low)
        self.south = site_id(high, z, core, (y + 3) % 4, low)
        self.inner = site_id(high, z, core, y, 1 - low)
        self.sibling = site_id(high, z, 1 - core, y, low)
        self.mine = self.slot(high, z)
        self.handed = ([], [], [])
        self.passed = []
        self.started = []

    def slot(self, half, level):
        return half * 16 + level % 8 * 2 + self.place[2]

    def copy(self, kind, which, peer, index, half=None):
        first, last = CHUNKS[kind]
        if half is not None:
            middle = (first + last) // 2
            first, last = (first, middle) if half == 0 else (middle, last)
        piece = self.blocks.at[which, first:last]
        return remote(
            piece, piece, self.send_sem.at[index, kind], self.recv_sem.at[index, kind], peer
        )

    def send(self, kind, which, peer, index, half=None):
        copy = self.copy(kind, which, peer, index, half)
        copy.start()
        self.started.append(copy)

    def arrive(self, kind, which, peer, index, half=None):
        self.copy(kind, which, peer, index, half).wait_recv()

    def hand(self, kind, which):
        self.send(kind, which, self.sibling, HANDED + len(self.handed[kind]))
        self.handed[kind].append(which)

    def begin(self, kind):
        self.send(kind, self.mine, self.up, 0)
        self.send(kind, self.mine, self.down, 4)
        if kind == 0:
            self.pass_across(self.mine)
        self.hand(kind, self.mine)

    def pass_across(self, which):
        self.send(0, which, self.across, ACROSS + len(self.passed))
        self.passed.append(which)

    def hop(self, kind, hop):
        high, z, core, y, low = self.place
        half = (0, 1) if hop == 4 else (None, None)
        lower, upper = self.slot(high, z + 8 - hop), self.slot(high, z + hop)
        self.arrive(kind, lower, self.up, hop - 1, half[0])
        if hop < 4:
            self.send(kind, lower, self.up, hop, 0 if hop == 3 else None)
        self.arrive(kind, upper, self.down, 4 + hop - 1, half[1])
        if hop < 4:
            self.send(kind, upper, self.down, 4 + hop, 1 if hop == 3 else None)
        if kind == 0:
            for which in (lower, upper)[hop // 4 :]:
                self.pass_across(which)
        elif hop % 2 == 0:
            self.send(kind, self.brought(hop // 2 - 1, y, 1 - low, high), self.across, 7 + hop // 2)
        for which in (lower, upper)[hop // 4 :]:
            self.hand(kind, which)

    def finish_own(self, first, last):
        for index in range(first, last):
            which = self.passed[index]
            other = which + 16 - 32 * self.place[0]
            self.arrive(0, other, self.across, ACROSS + index)
            self.hand(0, other)

    def brought(self, far, y, low, half):
        return self.slot(half, self.place[1] + y % 2 * 2 + low + (3 if far else 7))

    def leg(self, kind, leg, far):
        high, z, core, y, low = self.place
        if leg == 0:
            which, index, peer = self.brought(far, y, low, 1 - high), 8, self.across
            onward = ((self.inner, 10), (self.north, 12))
        elif leg == 1:
            which, index, peer = self.brought(far, y, 1 - low, 1 - high), 10, self.inner
            onward = ((self.south, 14),)
        elif leg == 2:
            which, index, peer = self.brought(far, y + 1, low, 1 - high), 12, self.north
            onward = ()
        else:
            which, index, peer = self.brought(far, y + 1, 1 - low, 1 - high), 14, self.south
            onward = ()
        self.arrive(kind, which, peer, index + far)
        for target, number in onward:
            self.send(kind, which, target, number + far)
        self.hand(kind, which)

    def collect(self, kind):
        for index, which in enumerate(self.handed[kind]):
            self.arrive(kind, which + 1 - 2 * self.place[2], self.sibling, HANDED + index)

    def events(self):
        def hop(kind, number):
            return lambda: self.hop(kind, number)

        def leg(kind, number, far):
            return lambda: self.leg(kind, number, far)

        plan = [hop(1, 1), lambda: self.begin(2), hop(1, 2), hop(2, 1)]
        plan += [leg(1, 0, 0), hop(1, 3), hop(2, 2), leg(1, 1, 0), leg(1, 2, 0), hop(1, 4), hop(2, 3)]
        plan += [leg(2, 0, 0), hop(2, 4), leg(1, 3, 0), leg(2, 1, 0), leg(2, 2, 0), leg(1, 0, 1)]
        plan += [leg(2, 0, 1), leg(2, 3, 0), leg(1, 1, 1), leg(1, 2, 1), leg(2, 1, 1), leg(2, 2, 1)]
        plan += [leg(1, 3, 1), leg(2, 3, 1)]
        return plan


def pack_rows(blocks, mine, first, rest, tail, pieces):
    tile = 0
    for count, top, low in pieces:
        for number in range(count):
            blocks[mine, first + tile] = top(number)
            tail[0:4, tile * LANES : (tile + 1) * LANES] = low(number)
            tile += 1
    total = tail.shape[1] // LANES
    if total > tile:
        tail[0:4, tile * LANES :] = jnp.zeros((4, (total - tile) * LANES), jnp.float32)
    quarter = total // 4
    for number in range(quarter):
        rows = [
            tail[0:4, (a * quarter + number) * LANES : (a * quarter + number + 1) * LANES]
            for a in range(4)
        ]
        packed = jnp.concatenate(rows, 0).astype(jnp.bfloat16)
        blocks[mine, rest + number // 2, number % 2 * TILE : (number % 2 + 1) * TILE, :] = packed


def restore_rows(blocks, whole, first, rest, quarter, tiles):
    @pl.loop(0, 8)
    def _(quad):
        rows = pl.ds(pl.multiple_of(quad * 144, 16), 144)
        for tile in range(*tiles):
            a, number = tile // quarter, tile % quarter
            half = number % 2 * TILE
            pieces = []
            for device in range(4):
                which = quad * 4 + device
                pieces.append(blocks[which, first + tile].astype(jnp.float32))
                low = blocks[which, rest + number // 2, half : half + TILE, :].astype(jnp.float32)
                pieces.append(low[a * 4 : a * 4 + 4])
            joined = jnp.concatenate(pieces, 0)
            whole[rows, tile * LANES : (tile + 1) * LANES] = joined.astype(jnp.bfloat16)


def network_kernel(
    offsets, latents, facts, fresh, time_proj, embed_in, embed_out,
    proj_s, out_s, proj_t, out_t, queue, velocities,
    blocks, tail, own, shared, info, mods, tokens, mixed, parts, stage, landing,
    state, outgoing, back, again, triple, qs, ks, vs, mix,
    gather_send, gather_recv, fact_send, fact_recv, share_send, share_recv,
    part_send, part_recv, row_send, row_recv, swap_send, swap_recv,
):
    high, z, core, y, low = sites()
    place, row = y * 2 + low, lax.axis_index("frame")
    width, local_heads = HEADS * HEAD, HEADS // GROUPS
    span = local_heads * HEAD

    def plane_peer(dy, a, b, c):
        return site_id((high + b) % 2, z, (core + c) % 2, (y + dy) % 4, (low + a) % 2)

    offs = [(dy, a, b, c) for dy in range(4) for a in range(2) for b in range(2) for c in range(2)]
    above = [site_id(high, (z + d) % 8, core, y, low) for d in range(1, 8)]
    frames = [(h, d, c) for h in range(2) for d in range(1, 8) for c in range(2)]
    everyone_here = greet(
        [plane_peer(*offset) for offset in offs[1:]]
        + [site_id((high + h) % 2, (z + d) % 8, (core + c) % 2, y, low) for h, d, c in frames]
    )

    mine = pl.ds(pl.multiple_of(place * LANES, LANES), LANES)
    near = [(dy, a) for dy in range(4) for a in range(2)]
    later = []

    def share(step, source):
        flying = [None]
        for index, (dy, a) in enumerate(near[1:]):
            other = (y + dy) % 4 * 2 + (low + a) % 2
            copy = remote(
                source.at[(low + a) % 2],
                tokens.at[step, mine, :],
                share_send.at[step, index],
                share_recv.at[step, index],
                {"frame": row, "space": other},
            )
            copy.start()
            flying.append(copy)
            later.append(copy)
        tokens[step, mine, :] = source[low]
        return flying

    gather = Gather(blocks, gather_send, gather_recv)
    source = lax.broadcasted_iota(jnp.int32, (width, span), 0)
    target = lax.broadcasted_iota(jnp.int32, (width, span), 1)
    chosen = jnp.where(source == target + y * span, 1.0, 0.0).astype(jnp.bfloat16)
    own_rows = triple
    for part in range(3):
        own_rows[0:36, part * span : (part + 1) * span] = jnp.dot(
            proj_s[:, part * width : (part + 1) * width], chosen, preferred_element_type=jnp.float32
        )
    own_rows[0:36, 3 * span : 7 * LANES] = jnp.zeros((36, 7 * LANES - 3 * span), jnp.float32)

    def wide_piece(number):
        return own_rows[0:TOP, number * LANES : (number + 1) * LANES].astype(jnp.bfloat16)

    def wide_rest(number):
        return own_rows[TOP:36, number * LANES : (number + 1) * LANES]

    pack_rows(blocks, gather.mine, 1, 0, tail.at[:, : 8 * LANES], [(7, wide_piece, wide_rest)])
    everyone_here()
    gather.begin(0)
    shares = share(0, latents)

    def pieces(ref):
        return (
            ref.shape[1] // LANES,
            lambda number: ref[:TOP, number * LANES : (number + 1) * LANES],
            lambda number: ref[TOP:, number * LANES : (number + 1) * LANES].astype(jnp.float32),
        )

    pack_rows(blocks, gather.mine, 14, 8, tail, [pieces(out_s), pieces(proj_t), pieces(out_t)])

    plan = gather.events()

    def advance(count):
        for _ in range(min(count, len(plan))):
            plan.pop(0)()

    gather.begin(1)
    gather.hop(0, 1)
    gather.hop(0, 2)
    advance(2)
    gather.hop(0, 3)
    gather.hop(0, 4)
    gather.finish_own(0, 5)
    advance(2)
    gather.finish_own(5, 8)
    gather.collect(0)
    restore_rows(blocks, own, 1, 0, 2, (0, 7))
    features = jnp.where(low == 0, facts[0:1, LANES:], facts[1:2, LANES:])
    features = jnp.broadcast_to(features, (SUB, 2 * LANES)).astype(jnp.bfloat16)
    first_mods = jnp.dot(features, time_proj[:, : 2 * width], preferred_element_type=jnp.float32)
    shift, scale = first_mods[:1, :width], 1.0 + first_mods[:1, width:]
    mixed[:, :, span:] = jnp.zeros((STEPS, 8 * LANES, 3 * LANES - span), jnp.bfloat16)

    def spatial(step, shares, between):
        for dy in range(4):
            for a in range(2):
                if (dy, a) != (0, 0):
                    shares[near.index((-dy % 4, a))].wait_recv()
            here = pl.ds(pl.multiple_of((y + dy) % 4 * BLOCK, BLOCK), BLOCK)
            hidden = jnp.dot(
                tokens[step, here, :PATCH], embed_in[...], preferred_element_type=jnp.float32
            )
            normed = layer_norm(hidden) * scale + shift
            triple[:, : 7 * LANES] = jnp.dot(
                normed.astype(jnp.bfloat16), own[...], preferred_element_type=jnp.float32
            )
            for head in range(local_heads):
                query = triple[:, head * HEAD : (head + 1) * HEAD]
                key = triple[:, span + head * HEAD : span + (head + 1) * HEAD]
                value = triple[:, 2 * span + head * HEAD : 2 * span + (head + 1) * HEAD]
                qs[head, here, :] = (query * (head_scale(query) * SHARPEN)).astype(jnp.bfloat16)
                ks[head, here, :] = (key * head_scale(key)).astype(jnp.bfloat16)
                vs[head, here, :HEAD] = value.astype(jnp.bfloat16)
                vs[head, here, HEAD:] = one_column(BLOCK)
            between()
        sent = []
        own_part = pl.ds(pl.multiple_of((high * 4 + core * 2 + low) * 32, 32), 32)
        for dy in range(4):
            first = (y + dy) % 4 * BLOCK
            here = pl.ds(pl.multiple_of(first, BLOCK), BLOCK)
            for head in range(local_heads):
                raised = jnp.exp2(contract_last(qs[head, here, :], ks[head])).astype(jnp.bfloat16)
                part = jnp.dot(raised, vs[head], preferred_element_type=jnp.float32)
                part = part[:, :HEAD] / part[:, HEAD : HEAD + 1]
                mixed[step, here, head * HEAD : (head + 1) * HEAD] = part.astype(jnp.bfloat16)
            for index, (way, a, b, c) in enumerate(offs):
                if way != dy:
                    continue
                target = (low + a) % 2 * 4 + (high + b) % 2 * 2 + (core + c) % 2
                piece = pl.ds(pl.multiple_of(first + target * 32, 32), 32)
                if index == 0:
                    parts[step, y, own_part, :] = mixed[step, piece, :]
                    continue
                copy = remote(
                    mixed.at[step, piece, :],
                    parts.at[step, y, own_part, :],
                    part_send.at[step, index - 1],
                    part_recv.at[step, index - 1],
                    plane_peer(way, a, b, c),
                )
                copy.start()
                sent.append(copy)
            between()
        between()
        for copy in sent:
            copy.wait_recv()
        later.extend(sent)
        target = lax.broadcasted_iota(jnp.int32, (2 * LANES, 2 * LANES), 0)
        source = lax.broadcasted_iota(jnp.int32, (2 * LANES, 2 * LANES), 1)
        moved = target % 32 // 8 * 64 + target % 2 * 32 + target // 32 * 4 + target % 8 // 2
        order = jnp.where(moved == source, 1.0, 0.0).astype(jnp.bfloat16)
        for group in range(GROUPS):
            piece = jnp.dot(order, parts[step, group], preferred_element_type=jnp.float32)
            stage[step, :, group * span : (group + 1) * span] = piece[:, :span].astype(jnp.bfloat16)
        flying = []
        for d in range(1, 8):
            for half in range(2):
                origin = pl.ds(pl.multiple_of((z + d) % 8 * 32 + half * TILE, TILE), TILE)
                goal = pl.ds(pl.multiple_of(half * LANES + z * TILE, TILE), TILE)
                copy = remote(
                    stage.at[step, origin, :],
                    landing.at[step, goal, :],
                    row_send.at[step, d - 1, half],
                    row_recv.at[step, d - 1, half],
                    above[d - 1],
                )
                copy.start()
                flying.append(copy)
        for half in range(2):
            origin = pl.ds(pl.multiple_of(z * 32 + half * TILE, TILE), TILE)
            goal = pl.ds(pl.multiple_of(half * LANES + z * TILE, TILE), TILE)
            landing[step, goal, :] = stage[step, origin, :]
        later.extend(flying)
        return flying

    rows = 2 * LANES

    def temporal_head(step):
        hidden_in = jnp.dot(
            state[:, :PATCH].astype(jnp.bfloat16), embed_in[...], preferred_element_type=jnp.float32
        )
        out = jnp.dot(landing[step], shared[:, :width], preferred_element_type=jnp.float32)
        hidden = hidden_in + mods[0] * out
        normed = layer_norm(hidden) * (1.0 + mods[2]) + mods[1]
        mix[...] = normed.astype(jnp.bfloat16)
        return hidden

    def temporal(step, hidden):
        triple[...] = jnp.dot(
            mix[...], shared[:, width : 4 * width], preferred_element_type=jnp.float32
        )

        def place_of(index):
            frame = index // SUB * 2 + index % 2
            return (frame + WIN - offsets[step]) // WIN * SUB + index % SUB // 2

        same = place_of(lax.broadcasted_iota(jnp.int32, (rows, 1), 0)) == place_of(
            lax.broadcasted_iota(jnp.int32, (1, rows), 1)
        )
        ones = one_column(rows)
        for head in range(HEADS):
            query = triple[:, head * HEAD : (head + 1) * HEAD]
            key = triple[:, width + head * HEAD : width + (head + 1) * HEAD]
            value = triple[:, 2 * width + head * HEAD : 2 * width + (head + 1) * HEAD]
            query = (query * (head_scale(query) * SHARPEN)).astype(jnp.bfloat16)
            key = (key * head_scale(key)).astype(jnp.bfloat16)
            value = jnp.concatenate([value.astype(jnp.bfloat16), ones], -1)
            raised = jnp.where(same, jnp.exp2(contract_last(query, key)), 0.0)
            part = jnp.dot(raised.astype(jnp.bfloat16), value, preferred_element_type=jnp.float32)
            part = part[:, :HEAD] / part[:, HEAD : HEAD + 1]
            mix[:, head * HEAD : (head + 1) * HEAD] = part.astype(jnp.bfloat16)
        out = jnp.dot(mix[...], shared[:, 4 * width :], preferred_element_type=jnp.float32)
        hidden = hidden + mods[3] * out
        velocity = contract_last(layer_norm(hidden).astype(jnp.bfloat16), embed_out[...])
        return state[:, :PATCH] + info[:, PATCH : PATCH + 1] * velocity, velocity

    pace = [1, 2, 1, 1, 2, 1, 1, 1, 2]
    fact_copies = swap_rows(facts, info, fact_send, fact_recv)
    waiting = list(fact_copies)

    def between():
        for _ in range(min(5, len(waiting))):
            waiting.pop(0).start()
        advance(pace.pop(0))

    flying = spatial(0, shares, between)
    for copy in fact_copies:
        copy.wait_recv()
    later.extend(fact_copies)
    facts_rows = info[:, LANES:].astype(jnp.bfloat16)
    for part in range(4):
        columns = time_proj[:, (part + 2) * width : (part + 3) * width]
        mods[part] = jnp.dot(facts_rows, columns, preferred_element_type=jnp.float32)
    state[...] = info[:, :LANES]
    advance(len(plan) - 1)
    gather.collect(1)
    restore_rows(blocks, shared, 14, 8, 12, (0, 19))
    for copy in flying:
        copy.wait_recv()
    hidden = temporal_head(0)
    advance(1)
    gather.collect(2)
    restore_rows(blocks, shared, 14, 8, 12, (19, 45))
    stepped, velocity = temporal(0, hidden)
    outgoing[...] = jnp.zeros((STEPS, rows, LANES), jnp.float32)
    outgoing[0, :, :PATCH] = stepped
    wide = outgoing[0]
    index = lax.broadcasted_iota(jnp.int32, (rows, LANES), 0)
    first = index % 2 == 0
    ahead = jnp.where(first, pltpu.roll(wide, rows - 1, 0), pltpu.roll(wide, rows - 7, 0))
    added = jnp.concatenate([fresh[...]] * (rows // SUB), 0)
    ahead = jnp.where(first | (index < rows - SUB), ahead, added)
    outgoing[0] = ahead
    flying = swap_rows(outgoing.at[0], back.at[0], swap_send.at[0], swap_recv.at[0])
    for copy in flying:
        copy.start()
    later.extend(flying)
    state[:, :PATCH] = ahead[:, :PATCH]
    state[:, PATCH : 2 * PATCH] = velocity
    target = lax.broadcasted_iota(jnp.int32, (LANES, rows), 0)
    source = lax.broadcasted_iota(jnp.int32, (LANES, rows), 1)
    moved = target // 64 * 16 + target % 32 // 4 * 2 + target // 32 % 2
    moved = moved * SUB + target % 4 * 2
    for copy in flying:
        copy.wait_recv()
    arrived = back[0].astype(jnp.bfloat16)
    for j in range(2):
        order = jnp.where(moved + j == source, 1.0, 0.0).astype(jnp.bfloat16)
        piece = jnp.dot(order, arrived, preferred_element_type=jnp.float32)
        again[j] = piece.astype(jnp.bfloat16)
    shares = share(1, again)
    flying = spatial(1, shares, lambda: None)
    for copy in gather.started + later:
        copy.wait_send()
    for copy in flying:
        copy.wait_recv()
    stepped, velocity = temporal(1, temporal_head(1))
    outgoing[1, :, :PATCH] = stepped
    outgoing[1, :, PATCH : 2 * PATCH] = state[:, PATCH : 2 * PATCH]
    outgoing[1, :, 2 * PATCH : 3 * PATCH] = velocity
    flying = swap_rows(outgoing.at[1], back.at[1], swap_send.at[1], swap_recv.at[1])
    for copy in flying:
        copy.start()
    for copy in flying:
        copy.wait()
    for j in range(2):
        piece = jnp.transpose(back[1, pl.ds(j, LANES, stride=2), :])
        queue[j] = piece[:PATCH]
        velocities[0, j] = piece[PATCH : 2 * PATCH]
        velocities[1, j] = piece[2 * PATCH : 3 * PATCH]


def network(offsets, *arrays):
    width, local_heads, rows = HEADS * HEAD, HEADS // GROUPS, 2 * LANES
    vmem = pl.BlockSpec(memory_space=pltpu.VMEM)
    shape = (2, PATCH, LANES)
    bf16, f32, dma = jnp.bfloat16, jnp.float32, pltpu.SemaphoreType.DMA
    return pl.pallas_call(
        network_kernel,
        out_shape=[
            jax.ShapeDtypeStruct(shape, f32),
            jax.ShapeDtypeStruct((STEPS, *shape), f32),
        ],
        in_specs=[pl.BlockSpec(memory_space=pltpu.SMEM)] + [vmem] * len(arrays),
        out_specs=[vmem] * 2,
        scratch_shapes=[
            pltpu.VMEM((32, CHUNKS[-1][1], TOP, LANES), bf16),
            pltpu.VMEM((SUB, 48 * LANES), f32),
            pltpu.VMEM((width, 7 * LANES), bf16),
            pltpu.VMEM((width, 5 * width), bf16),
            pltpu.VMEM((rows, 3 * LANES), f32),
            pltpu.VMEM((4, rows, width), f32),
            pltpu.VMEM((STEPS, 8 * LANES, LANES), bf16),
            pltpu.VMEM((STEPS, 8 * LANES, 3 * LANES), bf16),
            pltpu.VMEM((STEPS, GROUPS, rows, 3 * LANES), bf16),
            pltpu.VMEM((STEPS, rows, width), bf16),
            pltpu.VMEM((STEPS, rows, width), bf16),
            pltpu.VMEM((rows, LANES), f32),
            pltpu.VMEM((STEPS, rows, LANES), f32),
            pltpu.VMEM((STEPS, rows, LANES), f32),
            pltpu.VMEM((2, LANES, LANES), bf16),
            pltpu.VMEM((rows, 3 * width), f32),
            pltpu.VMEM((local_heads, 8 * LANES, HEAD), bf16),
            pltpu.VMEM((local_heads, 8 * LANES, HEAD), bf16),
            pltpu.VMEM((local_heads, 8 * LANES, LANES), bf16),
            pltpu.VMEM((rows, width), bf16),
            dma((40, 3)), dma((40, 3)), dma((31,)), dma((31,)), dma((STEPS, 7)), dma((STEPS, 7)),
            dma((STEPS, 31)), dma((STEPS, 31)), dma((STEPS, 7, 2)), dma((STEPS, 7, 2)),
            dma((STEPS, 31)), dma((STEPS, 31)),
        ],
        compiler_params=pltpu.CompilerParams(
            collective_id=0, has_side_effects=True, vmem_limit_bytes=VMEM_BYTES
        ),
        name="network",
    )(offsets, *arrays)


def row_facts(latents, step_size, features):
    count, tokens, size = latents.shape
    rows = latents.reshape(count, 32, tokens // 32, size)
    rows = jnp.transpose(rows, (1, 2, 0, 3)).reshape(2 * tokens, size)
    steps = jnp.broadcast_to(step_size[None], (tokens, count)).reshape(2 * tokens, 1)
    wide = jnp.broadcast_to(features.astype(jnp.float32)[None], (tokens, count, 2 * LANES))
    gap = jnp.zeros((2 * tokens, LANES - size - 1), jnp.float32)
    return jnp.concatenate([rows, steps, gap, wide.reshape(2 * tokens, 2 * LANES)], -1)


def plane_rows(latents):
    rows = latents.astype(jnp.bfloat16).reshape(2, 2, 8, 2, 4, PATCH)
    rows = jnp.swapaxes(rows, 2, 3).reshape(2, LANES, PATCH)
    return jnp.pad(rows, ((0, 0), (0, 0), (0, LANES - PATCH)))


def local(
    latents,
    fresh_noise,
    levels,
    timesteps,
    window_offsets,
    time_proj,
    embed_in,
    spatial_proj,
    spatial_out,
    temporal_proj,
    temporal_out,
    embed_out,
):
    row = lax.axis_index("frame")
    time_value = lookup_table(levels, timesteps)
    earlier = lookup_table(levels - 1, timesteps)
    features = time_features(time_value, time_proj.shape[0] // 2)
    facts = row_facts(latents, (earlier - time_value) / 1000.0, features)
    fresh = lax.dynamic_slice_in_dim(fresh_noise[0], row * 4, 4)
    fresh = jnp.pad(jnp.repeat(fresh, 2, axis=0), ((0, 0), (0, LANES - PATCH)))
    queue, velocities = network(
        window_offsets,
        plane_rows(latents),
        facts,
        fresh,
        time_proj,
        embed_in,
        embed_out.T,
        spatial_proj,
        spatial_out,
        temporal_proj,
        temporal_out,
    )
    return jnp.swapaxes(queue, 1, 2), jnp.swapaxes(velocities, 2, 3)


def solution(mesh):
    return jax.shard_map(
        local,
        mesh=mesh,
        in_specs=(
            P("frame", "space", None),
            P(None, "space", None),
            P("frame"),
            P(),
            P(),
            P(),
            P(),
            P("frame", None),
            P("frame", None),
            P("frame", None),
            P("frame", None),
            P(),
        ),
        out_specs=(P("frame", "space", None), P(None, "frame", "space", None)),
        check_vma=False,
    )
```
